32 devices in a mesh: wide: 8 (over z, x), narrow: 4 (over y, core).
Axes of the slice: x: 2, y: 2, z: 4, core: 2. Of those that a mesh axis runs over, the one named last changes fastest.
Arguments:
- cell_tokens: bfloat16 [32, 2208, 256], P('wide'), may hold values from -6 to 6
- library_size: int32 [32], P('wide'), may hold values from 1000 to 19999
- gene_counts: int32 [32, 2200], P('wide'), may hold values from 0 to 7
- attend_in: float32 [3, 256, 256], P(None, None, 'narrow'), as said below
- attend_out: float32 [256, 256], P('narrow'), as said below
- up_weight: float32 [256, 1024], P(None, 'narrow'), as said below
- down_weight: float32 [1024, 256], P('narrow'), as said below
- norm_params: float32 [4, 256], replicated, as said below
- head_weight: float32 [3, 256], replicated, as said below
- first_in: float32 [3, 256, 256], P(None, None, 'narrow'), may hold values from -0.00018310547 to 0.00018310547
- first_out: float32 [256, 256], P('narrow'), may hold values from -0.00018310547 to 0.00018310547
- first_up: float32 [256, 1024], P(None, 'narrow'), may hold values from -0.00018310547 to 0.00018310547
- first_down: float32 [1024, 256], P('narrow'), may hold values from -0.00018310547 to 0.00018310547
- first_norm: float32 [4, 256], replicated, may hold values from -0.00048828125 to 0.00048828125
- first_head: float32 [3, 256], replicated, may hold values from -0.00048828125 to 0.00048828125
- second_in: float32 [3, 256, 256], P(None, None, 'narrow'), may hold values from 7.9292184e-11 to 3.1716874e-10
- second_out: float32 [256, 256], P('narrow'), may hold values from 7.9292184e-11 to 3.1716874e-10
- second_up: float32 [256, 1024], P(None, 'narrow'), may hold values from 7.9292184e-11 to 3.1716874e-10
- second_down: float32 [1024, 256], P('narrow'), may hold values from 7.9292184e-11 to 3.1716874e-10
- second_norm: float32 [4, 256], replicated, may hold values from 6.3433747e-10 to 2.5373499e-09
- second_head: float32 [3, 256], replicated, may hold values from 6.3433747e-10 to 2.5373499e-09
- average_in: float32 [3, 256, 256], P(None, 'wide', 'narrow'), may hold values from -0.375 to 0.375
- average_out: float32 [256, 256], P('narrow', 'wide'), may hold values from -0.375 to 0.375
- average_up: float32 [256, 1024], P('wide', 'narrow'), may hold values from -0.375 to 0.375
- average_down: float32 [1024, 256], P('narrow', 'wide'), may hold values from -0.1875 to 0.1875
- average_norm: float32 [4, 256], P(None, 'wide'), may hold values from 0.5 to 1.5
- average_head: float32 [3, 256], P(None, 'wide'), may hold values from -0.375 to 0.375
Outputs:
- output: bfloat16 [32, 2208, 256], P('wide')
- input_grad: float32 [32, 2208, 256], P('wide')
- grad_norm: float32 [], replicated
- clipped_in: float32 [3, 256, 256], P(None, None, 'narrow')
- new_first_in: float32 [3, 256, 256], P(None, None, 'narrow')
- new_second_in: float32 [3, 256, 256], P(None, None, 'narrow')
- new_attend_in: float32 [3, 256, 256], P(None, None, 'narrow')
- new_average_in: float32 [3, 256, 256], P(None, 'wide', 'narrow')
- clipped_out: float32 [256, 256], P('narrow')
- new_first_out: float32 [256, 256], P('narrow')
- new_second_out: float32 [256, 256], P('narrow')
- new_attend_out: float32 [256, 256], P('narrow')
- new_average_out: float32 [256, 256], P('narrow', 'wide')
- clipped_up: float32 [256, 1024], P(None, 'narrow')
- new_first_up: float32 [256, 1024], P(None, 'narrow')
- new_second_up: float32 [256, 1024], P(None, 'narrow')
- new_up_weight: float32 [256, 1024], P(None, 'narrow')
- new_average_up: float32 [256, 1024], P('wide', 'narrow')
- clipped_down: float32 [1024, 256], P('narrow')
- new_first_down: float32 [1024, 256], P('narrow')
- new_second_down: float32 [1024, 256], P('narrow')
- new_down_weight: float32 [1024, 256], P('narrow')
- new_average_down: float32 [1024, 256], P('narrow', 'wide')
- clipped_norm: float32 [4, 256], replicated
- new_first_norm: float32 [4, 256], replicated
- new_second_norm: float32 [4, 256], replicated
- new_norm_params: float32 [4, 256], replicated
- new_average_norm: float32 [4, 256], P(None, 'wide')
- clipped_head: float32 [3, 256], replicated
- new_first_head: float32 [3, 256], replicated
- new_second_head: float32 [3, 256], replicated
- new_head_weight: float32 [3, 256], replicated
- new_average_head: float32 [3, 256], P(None, 'wide')
The draws below stay inside these ranges and needn't reach their ends.
Inputs may be any that keep to these rules, and one draw needn't show every extreme that they name: `attend_in`: real values. `attend_out`: real values. `up_weight`: real values. `down_weight`: real values. `norm_params`: gains in rows 0 and 2 are positive. `head_weight`: real values.
All inputs are finite; a program needn't handle non-finite values.
Results may differ from the reference program's by a relative error of at most 0.017.
The reference program's roundings to bfloat16 on the way count: a program that leaves them out, or rounds other values in their place, can miss the bound.
Values may be sent and summed in bfloat16 or wider, within the bound.
A program may use at most 192 MiB of HBM per device.

```python
import math
import jax
import jax.numpy as jnp
from jax import lax

D = 256
FF = 1024
HEADS = 4
HEAD_DIM = 64
GENES = 2200
CLASS_TOK = 8
QBLOCKS = 4
STEP = 10
CELLS = 32


def rise_line(count, start, finish):
    return start + (finish - start) * jnp.arange(count, dtype=jnp.float32) / max(count - 1, 1)


def rough_base(key, shape, spread):
    return jax.random.truncated_normal(key, -4.0, 4.0, shape, jnp.float32) * spread


def draw_attend_in(key, part):
    key = jax.random.fold_in(key, 11)
    slope = rise_line(D, 0.6, 1.8)
    base = rough_base(key, (3, D, D), D ** (-0.5))
    return base * slope[None, None, :]


def draw_attend_out(key, part):
    key = jax.random.fold_in(key, 12)
    spread = ((GENES + CLASS_TOK) / (3.0 * D)) ** 0.5 / (1.2 * D ** 0.5)
    slope = rise_line(D, 0.6, 1.8)
    base = rough_base(key, (D, D), spread)
    return base * slope[:, None]


def draw_up_weight(key, part):
    key = jax.random.fold_in(key, 13)
    slope = rise_line(FF, 0.6, 1.8)
    base = rough_base(key, (D, FF), D ** (-0.5))
    return base * slope[None, :]


def draw_down_weight(key, part):
    key = jax.random.fold_in(key, 14)
    slope = rise_line(FF, 0.6, 1.8)
    base = rough_base(key, (FF, D), FF ** (-0.5))
    return base * slope[:, None]


def draw_norm_params(key, part):
    key = jax.random.fold_in(key, 15)
    gain_key, shift_key = jax.random.split(key)
    slope = rise_line(D, 0.6, 1.8)[None, :]
    gains = slope * (1.0 + rough_base(gain_key, (2, D), 0.1))
    shifts = rough_base(shift_key, (2, D), 0.3)
    return jnp.stack([gains[0], shifts[0], gains[1], shifts[1]])


def draw_head_weight(key, part):
    key = jax.random.fold_in(key, 16)
    slope = rise_line(D, 0.6, 1.8)
    base = rough_base(key, (3, D), D ** (-0.5))
    return base * slope[None, :]


def touch_ends(values, key, least, top_value):
    longest = values.shape.index(max(values.shape))
    spots = []
    for shift in (0, 1):
        where = [jax.random.randint(jax.random.fold_in(key, axis), (), 0, length) for axis, length in enumerate(values.shape)]
        where[longest] = (where[longest] + shift) % values.shape[longest]
        spots.append(tuple(where))
    return values.at[spots[0]].set(least).at[spots[1]].set(top_value)


def block_levels(key, dims, shards, smallest, high):
    loudness = 1.0
    for position, shards_of in shards:
        steps = jax.random.uniform(jax.random.fold_in(jax.random.fold_in(key, 6), position), (shards_of,), jnp.float32, smallest / len(shards), high / len(shards))
        loudness = loudness * jnp.repeat(jnp.exp(steps), dims[position] // shards_of).reshape((-1,) + (1,) * (len(dims) - 1 - position))
    return loudness


def scatter_about(own_key, extent, deviation, most, pieces=(), held_as=jnp.bfloat16):
    entries = jax.random.normal(own_key, extent, jnp.float32) * deviation
    if len(pieces) > 0:
        entries = block_levels(own_key, extent, pieces, -0.22, 0.18) * entries
    return jnp.clip(entries, min=-most, max=most).astype(held_as)


def setup_inputs(seed: int = 0) -> dict:
    splits = jax.random.split(jax.random.key(seed), 28)
    return {
        "cell_tokens": scatter_about(splits[0], (CELLS, GENES + CLASS_TOK, D), 1.0, 6.0, ((0, 8),)),
        "library_size": touch_ends(jax.random.randint(splits[1], (CELLS,), 1000, 20000), jax.random.fold_in(splits[1], 1), 1000, 19999).astype(jnp.int32),
        "gene_counts": touch_ends(jax.random.randint(splits[2], (CELLS, GENES), 0, 8), jax.random.fold_in(splits[2], 1), 0, 7).astype(jnp.int32),
        "attend_in": draw_attend_in(jax.random.fold_in(splits[27], 71), 0),
        "attend_out": draw_attend_out(jax.random.fold_in(splits[27], 71), 0),
        "up_weight": draw_up_weight(jax.random.fold_in(splits[27], 71), 0),
        "down_weight": draw_down_weight(jax.random.fold_in(splits[27], 71), 0),
        "norm_params": draw_norm_params(jax.random.fold_in(splits[27], 71), 0),
        "head_weight": draw_head_weight(jax.random.fold_in(splits[27], 71), 0),
        "first_in": scatter_about(splits[9], (3, D, D), (0.028 * (4 * D * D + 2 * D * FF + 7 * D) ** -0.5), 0.00018310547, ((2, 4),), jnp.float32),
        "first_out": scatter_about(splits[10], (D, D), (0.028 * (4 * D * D + 2 * D * FF + 7 * D) ** -0.5), 0.00018310547, ((0, 4),), jnp.float32),
        "first_up": scatter_about(splits[11], (D, FF), (0.028 * (4 * D * D + 2 * D * FF + 7 * D) ** -0.5), 0.00018310547, ((1, 4),), jnp.float32),
        "first_down": scatter_about(splits[12], (FF, D), (0.028 * (4 * D * D + 2 * D * FF + 7 * D) ** -0.5), 0.00018310547, ((0, 4),), jnp.float32),
        "first_norm": scatter_about(splits[13], (4, D), (0.08 * (4 * D * D + 2 * D * FF + 7 * D) ** -0.5), 0.00048828125, (), jnp.float32),
        "first_head": scatter_about(splits[14], (3, D), (0.08 * (4 * D * D + 2 * D * FF + 7 * D) ** -0.5), 0.00048828125, (), jnp.float32),
        "second_in": jnp.clip(jnp.exp(math.log(3.1716873571951965e-10) - 1.3862944 * jax.random.uniform(splits[15], (3, D, D), jnp.float32) ** block_levels(splits[15], (3, D, D), ((2, 4),), -0.2, 0.2)), 7.929218392987991e-11, 3.1716873571951965e-10),
        "second_out": jnp.clip(jnp.exp(math.log(3.1716873571951965e-10) - 1.3862944 * jax.random.uniform(splits[16], (D, D), jnp.float32) ** block_levels(splits[16], (D, D), ((0, 4),), -0.2, 0.2)), 7.929218392987991e-11, 3.1716873571951965e-10),
        "second_up": jnp.clip(jnp.exp(math.log(3.1716873571951965e-10) - 1.3862944 * jax.random.uniform(splits[17], (D, FF), jnp.float32) ** block_levels(splits[17], (D, FF), ((1, 4),), -0.2, 0.2)), 7.929218392987991e-11, 3.1716873571951965e-10),
        "second_down": jnp.clip(jnp.exp(math.log(3.1716873571951965e-10) - 1.3862944 * jax.random.uniform(splits[18], (FF, D), jnp.float32) ** block_levels(splits[18], (FF, D), ((0, 4),), -0.2, 0.2)), 7.929218392987991e-11, 3.1716873571951965e-10),
        "second_norm": jnp.clip(jnp.exp(jax.random.uniform(splits[19], (4, D), jnp.float32, math.log(6.343374714390393e-10), math.log(2.537349885756157e-09))), 6.343374714390393e-10, 2.537349885756157e-09),
        "second_head": jnp.clip(jnp.exp(jax.random.uniform(splits[20], (3, D), jnp.float32, math.log(6.343374714390393e-10), math.log(2.537349885756157e-09))), 6.343374714390393e-10, 2.537349885756157e-09),
        "average_in": scatter_about(splits[21], (3, D, D), D ** -0.5, 0.375, ((1, 8), (2, 4)), jnp.float32),
        "average_out": scatter_about(splits[22], (D, D), D ** -0.5, 0.375, ((0, 4), (1, 8)), jnp.float32),
        "average_up": scatter_about(splits[23], (D, FF), D ** -0.5, 0.375, ((0, 8), (1, 4)), jnp.float32),
        "average_down": scatter_about(splits[24], (FF, D), FF ** -0.5, 0.1875, ((0, 4), (1, 8)), jnp.float32),
        "average_norm": jnp.clip(1.0 + 0.1 * jax.random.normal(splits[25], (4, D), jnp.float32), 0.5, 1.5),
        "average_head": scatter_about(splits[26], (3, D), D ** -0.5, 0.375, ((1, 8),), jnp.float32),
    }


TOP_PRECISION = lax.Precision.HIGHEST
layer_eps = 1e-05
clip_limit = 0.25
decay_first = 0.9
decay_second = 0.999
learn_rate = 0.06
norm_rate = 0.6
adam_eps = 1e-08
weight_decay = 0.01
ema_keep = 0.75

@jax.custom_vjp
def low(v):
    return lax.optimization_barrier(v.astype(jnp.bfloat16)).astype(jnp.float32)

@jax.custom_vjp
def low_back(v):
    return v

def low_keep(v):
    return (low(v), None)

def low_pass(kept, grad):
    return (grad,)

def back_keep(v):
    return (v, None)

def back_low(kept, grad):
    return (low(grad),)
low.defvjp(low_keep, low_pass)
low_back.defvjp(back_keep, back_low)

def product(left, right):
    return jnp.dot(left, right, precision=TOP_PRECISION, preferred_element_type=jnp.float32)

def normalize(values, gain, shift):
    center = values - lax.optimization_barrier(jnp.mean(values, axis=-1, keepdims=True))
    spread = lax.optimization_barrier(jnp.mean(center * center, axis=-1, keepdims=True))
    return center * lax.rsqrt(spread + layer_eps) * gain + shift

def cell_nll(logits, counts, library):
    gene_row_block = logits[CLASS_TOK:]
    log_expected_mean = jax.nn.log_softmax(gene_row_block[:, 0]) + jnp.log(library.astype(jnp.float32))
    dispersion_shape = 0.5 + jax.nn.softplus(gene_row_block[:, 1])
    log_disp = jnp.log(dispersion_shape)
    zero_inflation_logit = gene_row_block[:, 2]
    log_mean_plus_dispersion = jnp.logaddexp(log_disp, log_expected_mean)
    observed_counts = counts.astype(jnp.float32)
    shared_tensors = dispersion_shape * (log_disp - log_mean_plus_dispersion)
    zero_count_term = jax.nn.softplus(-zero_inflation_logit) - jax.nn.softplus(shared_tensors - zero_inflation_logit)
    nonzero_count_term = zero_inflation_logit + jax.nn.softplus(-zero_inflation_logit) - shared_tensors - observed_counts * (log_expected_mean - log_mean_plus_dispersion) - lax.lgamma(observed_counts + dispersion_shape) + lax.lgamma(dispersion_shape) + lax.lgamma(observed_counts + 1.0)
    return jnp.mean(jnp.where(counts == 0, zero_count_term, nonzero_count_term))

def attend(query_rows, key_rows, value_rows):
    block_rows = query_rows.shape[0] // QBLOCKS

    def one_block(query_block):
        scores = low_back(product(query_block, key_rows.T) * HEAD_DIM ** (-0.5))
        row_max = lax.optimization_barrier(jnp.max(scores, axis=-1, keepdims=True))
        exp_scores = jnp.exp(scores - row_max)
        weight_tensors = exp_scores / lax.optimization_barrier(jnp.sum(exp_scores, axis=-1, keepdims=True))
        return product(low(weight_tensors), value_rows)
    outputs = lax.map(jax.checkpoint(one_block), query_rows.reshape(QBLOCKS, block_rows, HEAD_DIM))
    return outputs.reshape(-1, HEAD_DIM)

def cell_forward(stream, counts, library, params):
    attend_in, attend_out, up_weight, down_weight, norm_params, head_weight = params
    length = stream.shape[0]
    normed_one = normalize(stream, norm_params[0], norm_params[1])
    joined = low_back(low(jnp.einsum('ld,sde->sle', low(normed_one), low(attend_in), precision=TOP_PRECISION)))
    per_head = joined.reshape(3, length, HEADS, HEAD_DIM).transpose(0, 2, 1, 3)
    mixed = jax.vmap(attend)(per_head[0], per_head[1], per_head[2])
    mixed = low_back(low(mixed.transpose(1, 0, 2).reshape(length, D)))
    attended = low_back(product(mixed, low(attend_out)))
    middle = stream + attended
    normed_two = normalize(middle, norm_params[2], norm_params[3])
    before = low_back(product(low(normed_two), low(up_weight)))
    hidden = low(jax.nn.gelu(before))
    result = middle + low_back(product(hidden, low(down_weight)))
    logits = product(result, head_weight.T)
    return (cell_nll(logits, counts, library), result)

def adam_update(grad, first, second, weight, decay_rate, rate):
    first_new = decay_first * first + (1.0 - decay_first) * grad
    second_new = decay_second * second + (1.0 - decay_second) * grad * grad
    fix_first = 1.0 - decay_first ** STEP
    fix_second = 1.0 - decay_second ** STEP
    direction = first_new / fix_first / (jnp.sqrt(second_new / fix_second) + adam_eps)
    return (first_new, second_new, weight - rate * (direction + decay_rate * weight))

def reference(cell_tokens, library_size, gene_counts, attend_in, attend_out, up_weight, down_weight, norm_params, head_weight, first_in, first_out, first_up, first_down, first_norm, first_head, second_in, second_out, second_up, second_down, second_norm, second_head, average_in, average_out, average_up, average_down, average_norm, average_head):
    stream = cell_tokens.astype(jnp.float32)
    params = (attend_in, attend_out, up_weight, down_weight, norm_params, head_weight)

    def forward(inputs, weight_tensors):

        def one_cell(running, block_in):
            loss_cell, result = jax.checkpoint(cell_forward)(block_in[0], block_in[1], block_in[2], weight_tensors)
            return (running + loss_cell, result)
        return lax.scan(one_cell, jnp.zeros((), jnp.float32), (inputs, gene_counts, library_size))
    loss_value, pull, results = jax.vjp(forward, stream, params, has_aux=True)
    input_grad, grads = pull(jnp.ones((), jnp.float32))
    squares = jnp.zeros((), jnp.float32)
    for grad in grads:
        squares = squares + jnp.sum(grad * grad)
    grad_norm = jnp.sqrt(squares)
    factor = jnp.minimum(1.0, clip_limit / grad_norm)
    firsts = (first_in, first_out, first_up, first_down, first_norm, first_head)
    seconds = (second_in, second_out, second_up, second_down, second_norm, second_head)
    averages = (average_in, average_out, average_up, average_down, average_norm, average_head)
    decays = (weight_decay, weight_decay, weight_decay, weight_decay, 0.0, weight_decay)
    rates = (learn_rate, learn_rate, learn_rate, learn_rate, norm_rate, learn_rate)
    packed = []
    for index in range(6):
        clipped = grads[index] * factor
        first_new, second_new, weight_new = adam_update(clipped, firsts[index], seconds[index], params[index], decays[index], rates[index])
        average_new = ema_keep * averages[index] + (1.0 - ema_keep) * weight_new
        packed.append((clipped, first_new, second_new, weight_new, average_new))
    return (results.astype(jnp.bfloat16), input_grad, grad_norm, packed[0][0], packed[0][1], packed[0][2], packed[0][3], packed[0][4], packed[1][0], packed[1][1], packed[1][2], packed[1][3], packed[1][4], packed[2][0], packed[2][1], packed[2][2], packed[2][3], packed[2][4], packed[3][0], packed[3][1], packed[3][2], packed[3][3], packed[3][4], packed[4][0], packed[4][1], packed[4][2], packed[4][3], packed[4][4], packed[5][0], packed[5][1], packed[5][2], packed[5][3], packed[5][4])
```

```python
import functools

import jax
import jax.numpy as jnp
from jax import lax
from jax.experimental import pallas as pl
from jax.experimental.pallas import tpu as pltpu
from jax.sharding import PartitionSpec as P

D = 256
FF = 1024
HEADS = 4
HEAD_DIM = 64
CLASS_TOK = 8
STEP = 10

layer_eps = 1e-05
clip_limit = 0.25
decay_first = 0.9
decay_second = 0.999
learn_rate = 0.06
norm_rate = 0.6
adam_eps = 1e-08
weight_decay = 0.01
ema_keep = 0.75

f32 = jnp.float32
bf16 = jnp.bfloat16
HI = lax.Precision.HIGHEST

NN = (((1,), (0,)), ((), ()))
NT = (((1,), (1,)), ((), ()))
TN = (((0,), (0,)), ((), ()))

BLK = 256
PAIR = 2 * HEAD_DIM
WIDE_COLS = 2 * BLK
LOG2E = 1.4426950408889634
SCORE = LOG2E * HEAD_DIM ** (-0.5)
GELU_A = 0.7978845608028654
GELU_B = 0.044715
VMEM_BYTES = 60 * 2**20


def dot(left, right, dims=NN, precision=None):
    return lax.dot_general(left, right, dims, precision=precision, preferred_element_type=f32)


def ceil_to(value, unit):
    return -(-value // unit) * unit


def key_chunk(length):
    for rows in (368, 384, 256, 128, 64, 48, 32, 16):
        if length % rows == 0:
            return rows
    return length


def vmem(count):
    return [pl.BlockSpec(memory_space=pltpu.VMEM)] * count


def params():
    return pltpu.CompilerParams(vmem_limit_bytes=VMEM_BYTES)


def norm_parts(values):
    center = values - jnp.mean(values, axis=-1, keepdims=True)
    spread = jnp.mean(center * center, axis=-1, keepdims=True)
    inverse = lax.rsqrt(spread + layer_eps)
    return center * inverse, inverse


def norm_back(xhat, inverse, gain, grad):
    scaled = gain * grad
    mean_one = jnp.mean(scaled, axis=-1, keepdims=True)
    mean_two = jnp.mean(scaled * xhat, axis=-1, keepdims=True)
    return inverse * (scaled - mean_one - xhat * mean_two)


def row_sums(values):
    return jnp.sum(values.reshape(-1, 8, values.shape[-1]), axis=0)


def block_of(step, width=BLK):
    return pl.ds(pl.multiple_of(step * width, width), width)


def front_kernel(length, tok, w_in, w_in_t, npar, x1, k_nat, v_nat, q_nat, q_t, k_t, out_t, lse, xbuf, v_t, probs, qbd, sem):
    padded = x1.shape[0]
    blocks = padded // BLK
    rows = key_chunk(length)
    me = lax.axis_index("narrow")
    copy = pltpu.make_async_copy(tok.at[me], xbuf.at[pl.ds(0, length)], sem)
    copy.start()
    if padded > length:
        xbuf[length:, :] = jnp.zeros((padded - length, D), bf16)
        probs[length:, :] = jnp.zeros((padded - length, WIDE_COLS), bf16)
    qbd[...] = jnp.zeros(qbd.shape, bf16)
    lse[...] = jnp.zeros(lse.shape, f32)
    copy.wait()
    gain = npar[0:1, :]
    shift = npar[1:2, :]

    @pl.loop(0, blocks)
    def project(step):
        here = block_of(step)
        xhat, _ = norm_parts(xbuf[here, :].astype(f32))
        act = (xhat * gain + shift).astype(bf16)
        x1[here, :] = act
        q_nat[here, :] = dot(act, w_in[0]).astype(bf16)
        k_nat[here, :] = dot(act, w_in[1]).astype(bf16)
        v_nat[here, :] = dot(act, w_in[2]).astype(bf16)
        q_t[:, here] = dot(w_in_t[0], act, NT).astype(bf16)
        k_t[:, here] = dot(w_in_t[1], act, NT).astype(bf16)
        v_t[:, here] = dot(w_in_t[2], act, NT).astype(bf16)

    if padded > length:
        v_t[:, length:] = jnp.zeros((D, padded - length), bf16)

    def attend(shifted):
        for pair in range(HEADS // 2):
            low = pair * PAIR

            @pl.loop(0, blocks)
            def block(step):
                here = block_of(step)
                qbd[0:HEAD_DIM, 0:BLK] = q_t[low : low + HEAD_DIM, here]
                qbd[HEAD_DIM:PAIR, BLK:WIDE_COLS] = q_t[low + HEAD_DIM : low + PAIR, here]
                queries = qbd[...]

                def scores(start):
                    return dot(k_nat[start : start + rows, low : low + PAIR], queries) * SCORE

                top = jnp.zeros((1, WIDE_COLS), f32)
                if shifted:
                    top = jnp.full((1, WIDE_COLS), -jnp.inf, f32)
                    for start in range(0, length, rows):
                        top = jnp.maximum(top, jnp.max(scores(start), axis=0, keepdims=True))
                total = jnp.zeros((8, WIDE_COLS), f32)
                for start in range(0, length, rows):
                    score = scores(start)
                    weight = jnp.exp2(score - top) if shifted else jnp.exp2(score)
                    total = total + row_sums(weight)
                    probs[start : start + rows, :] = weight.astype(bf16)
                total = jnp.sum(total, axis=0, keepdims=True)
                mixed = dot(v_t[low : low + PAIR, :], probs[...])
                mixed = mixed / total
                out_t[low : low + HEAD_DIM, here] = mixed[0:HEAD_DIM, 0:BLK]
                out_t[low + HEAD_DIM : low + PAIR, here] = mixed[HEAD_DIM:PAIR, BLK:WIDE_COLS]
                log_total = top + jnp.log2(total)
                lse[2 * pair : 2 * pair + 1, here] = log_total[:, 0:BLK]
                lse[2 * pair + 1 : 2 * pair + 2, here] = log_total[:, BLK:WIDE_COLS]

    attend(False)
    level = lse[...]
    good = (level > -80.0) & (level < 120.0)
    wrong = jnp.max(jnp.where(good, 0.0, 1.0))

    @pl.when(wrong > 0.0)
    def again():
        attend(True)


def front(tokens, w_in, w_in_t, npar):
    length = tokens.shape[1]
    padded = ceil_to(length, BLK)
    shape = jax.ShapeDtypeStruct
    return pl.pallas_call(
        functools.partial(front_kernel, length),
        out_shape=(
            shape((padded, D), bf16),
            shape((padded, D), bf16),
            shape((padded, D), bf16),
            shape((padded, D), bf16),
            shape((D, padded), bf16),
            shape((D, padded), bf16),
            shape((D, padded), f32),
            shape((8, padded), f32),
        ),
        in_specs=[pl.BlockSpec(memory_space=pl.ANY)] + vmem(3),
        out_specs=tuple(vmem(8)),
        scratch_shapes=[
            pltpu.VMEM((padded, D), bf16),
            pltpu.VMEM((D, padded), bf16),
            pltpu.VMEM((padded, WIDE_COLS), bf16),
            pltpu.VMEM((PAIR, WIDE_COLS), bf16),
            pltpu.SemaphoreType.DMA,
        ],
        compiler_params=params(),
        name="front",
    )(tokens, w_in, w_in_t, npar)


def softplus(values):
    return jnp.maximum(values, 0.0) + jnp.log1p(jnp.exp(-jnp.abs(values)))


def sigmoid(values):
    return 1.0 / (1.0 + jnp.exp(-values))


def head_grads(logits, counts, library, genes, length):
    lane = lax.broadcasted_iota(jnp.int32, logits[0].shape, 1)
    valid = (lane >= CLASS_TOK) & (lane < length)
    mean_logit = jnp.where(valid, logits[0], -jnp.inf)
    top = jnp.max(mean_logit, axis=1, keepdims=True)
    raised = jnp.exp(mean_logit - top)
    total = jnp.sum(raised, axis=1, keepdims=True)
    share = raised / total
    log_mean = jnp.where(valid, logits[0], 0.0) - top - jnp.log(total) + jnp.log(library)
    disp = 0.5 + softplus(logits[1])
    log_disp = jnp.log(disp)
    inflate = logits[2]
    gap = log_mean - log_disp
    mean_part = sigmoid(gap)
    disp_part = sigmoid(-gap)
    log_both = jnp.maximum(log_disp, log_mean) + jnp.log1p(jnp.exp(-jnp.abs(gap)))
    shared = disp * (log_disp - log_both)
    shared_disp = (log_disp - log_both) + mean_part
    shared_mean = -disp * mean_part
    none = counts == 0.0
    lean = sigmoid(shared - inflate)
    psi = jnp.zeros_like(disp)
    for step in range(7):
        psi = psi + jnp.where(counts > step, 1.0 / (disp + step), 0.0)
    grad_disp = jnp.where(none, -lean * shared_disp, counts * disp_part / disp - shared_disp - psi)
    grad_mean = jnp.where(none, -lean * shared_mean, -shared_mean - counts * disp_part)
    grad_inflate = jnp.where(none, lean - sigmoid(-inflate), sigmoid(inflate))
    part = 1.0 / genes
    grad_disp = jnp.where(valid, grad_disp * part, 0.0)
    grad_mean = jnp.where(valid, grad_mean * part, 0.0)
    grad_inflate = jnp.where(valid, grad_inflate * part, 0.0)
    grad_zero = grad_mean - share * jnp.sum(grad_mean, axis=1, keepdims=True)
    return (grad_zero, grad_disp * sigmoid(logits[1]), grad_inflate)


def middle_kernel(
    length,
    tok,
    out_t,
    w_out,
    w_up,
    w_down,
    npar,
    head,
    counts,
    library,
    output,
    grad_mid,
    g_nat,
    g_t,
    delta,
    grad_down,
    grad_up,
    grad_out,
    grad_norm,
    grad_head,
    xbuf,
    mixed_t,
    mid,
    res,
    act,
    hidden,
    slope,
    res_low,
    grad_before,
    mid_low,
    logits,
    sem,
):
    padded = xbuf.shape[0]
    blocks = padded // BLK
    me = lax.axis_index("narrow")
    copy = pltpu.make_async_copy(tok.at[me], xbuf.at[pl.ds(0, length)], sem)
    copy.start()
    if padded > length:
        xbuf[length:, :] = jnp.zeros((padded - length, D), bf16)
    grad_norm[...] = jnp.zeros(grad_norm.shape, f32)
    grad_head[...] = jnp.zeros(grad_head.shape, f32)
    copy.wait()
    gain = npar[2:3, :]
    shift = npar[3:4, :]

    @pl.loop(0, blocks)
    def forward(step):
        here = block_of(step)
        mixed = out_t[:, here].astype(bf16)
        mixed_t[:, here] = mixed
        middle = xbuf[here, :].astype(f32) + dot(mixed, w_out[...], TN)
        mid[here, :] = middle
        xhat, _ = norm_parts(middle)
        low = (xhat * gain + shift).astype(bf16)
        act[here, :] = low
        before = dot(low, w_up[...])
        square = before * before
        bend = jnp.tanh(GELU_A * before * (1.0 + GELU_B * square))
        half = 0.5 + 0.5 * bend
        hid = (before * half).astype(bf16)
        hidden[here, :] = hid
        slope[here, :] = half + 0.5 * before * (1.0 - bend * bend) * (GELU_A + 3.0 * GELU_A * GELU_B * square)
        result = middle + dot(hid, w_down[...])
        res[here, :] = result
        logits[:, here] = dot(head[...], result, NT, HI)

    output[...] = res[0:length, :].astype(bf16)
    genes = length - CLASS_TOK
    zero, disp, inflate = head_grads(
        (logits[0:1, :], logits[1:2, :], logits[2:3, :]),
        counts[0:1, :].astype(f32),
        library[0:1, 0:1].astype(f32),
        genes,
        length,
    )
    logits[0:1, :] = zero
    logits[1:2, :] = disp
    logits[2:3, :] = inflate
    logits[3:8, :] = jnp.zeros((5, padded), f32)

    @pl.loop(0, blocks)
    def backward(step):
        here = block_of(step)
        down_logits = logits[:, here]
        grad_res = dot(down_logits, head[...], TN, HI)
        grad_head[...] += dot(down_logits, res[here, :], NN, HI)
        low = grad_res.astype(bf16)
        res_low[here, :] = low
        grad_hidden = dot(low, w_down[...], NT)
        back = (slope[here, :] * grad_hidden).astype(bf16)
        grad_before[here, :] = back
        grad_two = dot(back, w_up[...], NT)
        xhat, inverse = norm_parts(mid[here, :])
        grad_norm[0:8, :] += row_sums(grad_two * xhat)
        grad_norm[8:16, :] += row_sums(grad_two)
        total = grad_res + norm_back(xhat, inverse, gain, grad_two)
        mid[here, :] = total
        total_low = total.astype(bf16)
        mid_low[here, :] = total_low
        g_nat[here, :] = dot(total_low, w_out[...], NT).astype(bf16)
        grad_t = dot(w_out[...], total_low, NT).astype(bf16)
        g_t[:, here] = grad_t
        inner = grad_t.astype(f32) * out_t[:, here]
        delta[:, here] = jnp.concatenate(
            [
                jnp.sum(inner[h * HEAD_DIM : (h + 1) * HEAD_DIM], axis=0, keepdims=True)
                for h in range(HEADS)
            ]
            + [jnp.zeros((8 - HEADS, BLK), f32)],
            axis=0,
        )

    grad_mid[...] = mid[0:length, :]
    grad_down[...] = dot(res_low[...], hidden[...], TN)
    grad_up[...] = dot(act[...], grad_before[...], TN)
    grad_out[...] = dot(mixed_t[...], mid_low[...])


def middle_stage(tokens, out_t, w_out, w_up, w_down, npar, head, counts, library):
    length = tokens.shape[1]
    padded = out_t.shape[1]
    shape = jax.ShapeDtypeStruct
    return pl.pallas_call(
        functools.partial(middle_kernel, length),
        out_shape=(
            shape((length, D), bf16),
            shape((length, D), f32),
            shape((padded, D), bf16),
            shape((D, padded), bf16),
            shape((8, padded), f32),
            shape((D, FF), f32),
            shape((D, FF), f32),
            shape((D, D), f32),
            shape((16, D), f32),
            shape((8, D), f32),
        ),
        in_specs=[pl.BlockSpec(memory_space=pl.ANY)] + vmem(8),
        out_specs=tuple(vmem(10)),
        scratch_shapes=[
            pltpu.VMEM((padded, D), bf16),
            pltpu.VMEM((D, padded), bf16),
            pltpu.VMEM((padded, D), f32),
            pltpu.VMEM((padded, D), f32),
            pltpu.VMEM((padded, D), bf16),
            pltpu.VMEM((padded, FF), bf16),
            pltpu.VMEM((padded, FF), f32),
            pltpu.VMEM((padded, D), bf16),
            pltpu.VMEM((padded, FF), bf16),
            pltpu.VMEM((padded, D), bf16),
            pltpu.VMEM((8, padded), f32),
            pltpu.SemaphoreType.DMA,
        ],
        compiler_params=params(),
        name="middle",
    )(tokens, out_t, w_out, w_up, w_down, npar, head, counts, library)


def back_kernel(
    length,
    tok,
    x1,
    k_nat,
    v_nat,
    q_nat,
    q_t,
    k_t,
    g_nat,
    g_t,
    lse,
    delta,
    grad_mid,
    w_in,
    npar,
    grad_input,
    grad_in,
    grad_norm,
    xbuf,
    probs,
    dscore,
    qbd,
    gbd,
    qnd,
    gnd,
    dk,
    dv,
    dq_t,
    joined,
    sem,
):
    padded = x1.shape[0]
    blocks = padded // BLK
    rows = key_chunk(length)
    me = lax.axis_index("narrow")
    copy = pltpu.make_async_copy(tok.at[me], xbuf.at[pl.ds(0, length)], sem)
    copy.start()
    if padded > length:
        xbuf[length:, :] = jnp.zeros((padded - length, D), bf16)
        dscore[length:, :] = jnp.zeros((padded - length, WIDE_COLS), bf16)
        joined[1, length:, :] = jnp.zeros((padded - length, D), bf16)
        joined[2, length:, :] = jnp.zeros((padded - length, D), bf16)
    for ref in (qbd, gbd, qnd, gnd):
        ref[...] = jnp.zeros(ref.shape, bf16)
    grad_norm[...] = jnp.zeros(grad_norm.shape, f32)
    scale = HEAD_DIM ** (-0.5)

    for pair in range(HEADS // 2):
        low = pair * PAIR
        mid = low + HEAD_DIM
        top = low + PAIR
        dk[...] = jnp.zeros(dk.shape, f32)
        dv[...] = jnp.zeros(dv.shape, f32)

        @pl.loop(0, blocks)
        def block(step):
            here = block_of(step)
            qbd[0:HEAD_DIM, 0:BLK] = q_t[low:mid, here]
            qbd[HEAD_DIM:PAIR, BLK:WIDE_COLS] = q_t[mid:top, here]
            gbd[0:HEAD_DIM, 0:BLK] = g_t[low:mid, here]
            gbd[HEAD_DIM:PAIR, BLK:WIDE_COLS] = g_t[mid:top, here]
            both = q_nat[here, low:top]
            qnd[0:BLK, 0:HEAD_DIM] = both[:, 0:HEAD_DIM]
            qnd[BLK:WIDE_COLS, HEAD_DIM:PAIR] = both[:, HEAD_DIM:PAIR]
            both = g_nat[here, low:top]
            gnd[0:BLK, 0:HEAD_DIM] = both[:, 0:HEAD_DIM]
            gnd[BLK:WIDE_COLS, HEAD_DIM:PAIR] = both[:, HEAD_DIM:PAIR]
            queries = qbd[...]
            grads = gbd[...]
            level = jnp.concatenate([lse[2 * pair : 2 * pair + 1, here], lse[2 * pair + 1 : 2 * pair + 2, here]], axis=1)
            inner = jnp.concatenate(
                [delta[2 * pair : 2 * pair + 1, here], delta[2 * pair + 1 : 2 * pair + 2, here]], axis=1
            )
            for start in range(0, length, rows):
                part = slice(start, start + rows)
                weight = jnp.exp2(dot(k_nat[part, low:top], queries) * SCORE - level)
                probs[part, :] = weight.astype(bf16)
                change = dot(v_nat[part, low:top], grads) - inner
                dscore[part, :] = (weight * change).astype(bf16)
            dv[...] += dot(probs[...], gnd[...])
            dk[...] += dot(dscore[0:length, :], qnd[...])
            moved = dot(k_t[low:top, :], dscore[...]) * scale
            dq_t[low:mid, here] = moved[0:HEAD_DIM, 0:BLK].astype(bf16)
            dq_t[mid:top, here] = moved[HEAD_DIM:PAIR, BLK:WIDE_COLS].astype(bf16)

        joined[1, 0:length, low:top] = (dk[...] * scale).astype(bf16)
        joined[2, 0:length, low:top] = dv[...].astype(bf16)

    copy.wait()
    gain = npar[0:1, :]

    @pl.loop(0, blocks)
    def close(step):
        here = block_of(step)
        grad_q = dq_t[:, here].T
        joined[0, here, :] = grad_q
        total = dot(grad_q, w_in[0], NT) + dot(joined[1, here, :], w_in[1], NT) + dot(joined[2, here, :], w_in[2], NT)
        xhat, inverse = norm_parts(xbuf[here, :].astype(f32))
        grad_norm[0:8, :] += row_sums(total * xhat)
        grad_norm[8:16, :] += row_sums(total)
        grad_input[here, :] = grad_mid[here, :] + norm_back(xhat, inverse, gain, total)

    for which in range(3):
        grad_in[which] = dot(joined[which], x1[...], TN)


def back_stage(tokens, x1, k_nat, v_nat, q_nat, q_t, k_t, g_nat, g_t, lse, delta, grad_mid, w_in, npar):
    length = tokens.shape[1]
    padded = x1.shape[0]
    shape = jax.ShapeDtypeStruct
    return pl.pallas_call(
        functools.partial(back_kernel, length),
        out_shape=(
            shape((padded, D), f32),
            shape((3, D, D), f32),
            shape((16, D), f32),
        ),
        in_specs=[pl.BlockSpec(memory_space=pl.ANY)] + vmem(13),
        out_specs=tuple(vmem(3)),
        scratch_shapes=[
            pltpu.VMEM((padded, D), bf16),
            pltpu.VMEM((length, WIDE_COLS), bf16),
            pltpu.VMEM((padded, WIDE_COLS), bf16),
            pltpu.VMEM((PAIR, WIDE_COLS), bf16),
            pltpu.VMEM((PAIR, WIDE_COLS), bf16),
            pltpu.VMEM((WIDE_COLS, PAIR), bf16),
            pltpu.VMEM((WIDE_COLS, PAIR), bf16),
            pltpu.VMEM((length, PAIR), f32),
            pltpu.VMEM((length, PAIR), f32),
            pltpu.VMEM((D, padded), bf16),
            pltpu.VMEM((3, padded, D), bf16),
            pltpu.SemaphoreType.DMA,
        ],
        compiler_params=params(),
        name="back",
    )(tokens, x1, k_nat, v_nat, q_nat, q_t, k_t, g_nat, g_t, lse, delta, grad_mid, w_in, npar)


def adam_update(grad, first, second, weight, decay_rate, rate):
    first_new = decay_first * first + (1.0 - decay_first) * grad
    second_new = decay_second * second + (1.0 - decay_second) * grad * grad
    fix_first = 1.0 - decay_first**STEP
    fix_second = 1.0 - decay_second**STEP
    direction = first_new / fix_first / (jnp.sqrt(second_new / fix_second) + adam_eps)
    return (first_new, second_new, weight - rate * (direction + decay_rate * weight))


def average_update(average, weight_new, dim):
    count = average.shape[dim]
    piece = lax.dynamic_slice_in_dim(weight_new, lax.axis_index("wide") * count, count, dim)
    return ema_keep * average + (1.0 - ema_keep) * piece


def on_device(cell_tokens, library_size, gene_counts, *state):
    weights, firsts, seconds, averages = state[0:6], state[6:12], state[12:18], state[18:24]
    attend_in, attend_out, up_weight, down_weight, norm_params, head_weight = weights
    cells, length, _ = cell_tokens.shape
    padded = ceil_to(length, BLK)
    me = lax.axis_index("narrow")

    w_in = lax.all_gather(attend_in.astype(bf16), "narrow", axis=2, tiled=True)
    w_out = lax.all_gather(attend_out.astype(bf16), "narrow", axis=0, tiled=True)
    w_up = lax.all_gather(up_weight.astype(bf16), "narrow", axis=1, tiled=True)
    w_down = lax.all_gather(down_weight.astype(bf16), "narrow", axis=0, tiled=True)
    w_in_t = w_in.transpose(0, 2, 1)
    head = jnp.pad(head_weight, ((0, 5), (0, 0)))
    counts = lax.dynamic_slice_in_dim(gene_counts, me, 1, 0)
    counts = jnp.pad(counts, ((0, 0), (CLASS_TOK, padded - length)))
    library = lax.dynamic_slice_in_dim(library_size, me, 1, 0).reshape(1, 1)

    x1, k_nat, v_nat, q_nat, q_t, k_t, out_t, lse = front(cell_tokens, w_in, w_in_t, norm_params)
    out_own, grad_mid, g_nat, g_t, delta, grad_down, grad_up, grad_out, norm_two, grad_head = middle_stage(
        cell_tokens, out_t, w_out, w_up, w_down, norm_params, head, counts, library
    )
    output = lax.all_gather(out_own, "narrow")
    grad_mid = jnp.pad(grad_mid, ((0, padded - length), (0, 0)))
    grad_input, grad_in, norm_one = back_stage(
        cell_tokens, x1, k_nat, v_nat, q_nat, q_t, k_t, g_nat, g_t, lse, delta, grad_mid, w_in, norm_params
    )
    input_grad = lax.all_gather(grad_input[:length].astype(bf16), "narrow").astype(f32)

    narrow = lax.axis_size("narrow")
    shard = lambda v, dim: lax.psum(lax.psum_scatter(v, "narrow", scatter_dimension=dim, tiled=True), "wide")
    grad_in = shard(grad_in.transpose(0, 2, 1), 2)
    grad_out = shard(grad_out, 0)
    grad_up = shard(grad_up, 1)
    grad_down = shard(grad_down.T, 0)
    fold = lambda v: jnp.stack([jnp.sum(v[0:8], axis=0), jnp.sum(v[8:16], axis=0)])
    grad_norms, grad_head = lax.psum(
        (jnp.concatenate([fold(norm_one), fold(norm_two)], axis=0), grad_head[0:3]), ("wide", "narrow")
    )
    sharded = (
        jnp.sum(grad_in * grad_in)
        + jnp.sum(grad_out * grad_out)
        + jnp.sum(grad_up * grad_up)
        + jnp.sum(grad_down * grad_down)
    )
    common = jnp.sum(grad_norms * grad_norms) + jnp.sum(grad_head * grad_head)
    grad_norm = jnp.sqrt(lax.psum(sharded, "narrow") + common)
    factor = jnp.minimum(1.0, clip_limit / grad_norm)
    grads = (grad_in, grad_out, grad_up, grad_down, grad_norms, grad_head)
    decays = (weight_decay,) * 4 + (0.0, weight_decay)
    rates = (learn_rate,) * 4 + (norm_rate, learn_rate)
    dims = (1, 1, 0, 1, 1, 1)
    outs = [output, input_grad, grad_norm]
    for index in range(6):
        clipped = grads[index] * factor
        first_new, second_new, weight_new = adam_update(
            clipped, firsts[index], seconds[index], weights[index], decays[index], rates[index]
        )
        outs += [clipped, first_new, second_new, weight_new, average_update(averages[index], weight_new, dims[index])]
    return tuple(outs)


def solution(mesh):
    by_in, by_rows, by_cols = P(None, None, "narrow"), P("narrow", None), P(None, "narrow")
    kinds = (by_in, by_rows, by_cols, by_rows, P(), P())
    means = (
        P(None, "wide", "narrow"),
        P("narrow", "wide"),
        P("wide", "narrow"),
        P("narrow", "wide"),
        P(None, "wide"),
        P(None, "wide"),
    )
    cell = P("wide", None, None)
    outs = (cell, cell, P())
    for kind, mean in zip(kinds, means):
        outs += (kind, kind, kind, kind, mean)
    return jax.shard_map(
        on_device,
        mesh=mesh,
        in_specs=(cell, P("wide"), P("wide", None)) + kinds * 3 + means,
        out_specs=outs,
        check_vma=False,
    )
```

```python
import functools

import jax
import jax.numpy as jnp
from jax import lax
from jax.experimental import pallas as pl
from jax.experimental.pallas import tpu as pltpu
from jax.sharding import PartitionSpec as P

D = 256
FF = 1024
HEADS = 4
HEAD_DIM = 64
CLASS_TOK = 8
STEP = 10

layer_eps = 1e-05
clip_limit = 0.25
decay_first = 0.9
decay_second = 0.999
learn_rate = 0.06
norm_rate = 0.6
adam_eps = 1e-08
weight_decay = 0.01
ema_keep = 0.75

f32 = jnp.float32
bf16 = jnp.bfloat16
HI = lax.Precision.HIGHEST

NN = (((1,), (0,)), ((), ()))
NT = (((1,), (1,)), ((), ()))
TN = (((0,), (0,)), ((), ()))

BLK = 256
PAIR = 2 * HEAD_DIM
WIDE_COLS = 2 * BLK
LOG2E = 1.4426950408889634
SCORE = LOG2E * HEAD_DIM ** (-0.5)
GELU_A = 0.7978845608028654
GELU_B = 0.044715
VMEM_BYTES = 60 * 2**20


def dot(left, right, dims=NN, precision=None):
    return lax.dot_general(left, right, dims, precision=precision, preferred_element_type=f32)


def ceil_to(value, unit):
    return -(-value // unit) * unit


def key_chunk(length):
    for rows in (368, 384, 256, 128, 64, 48, 32, 16):
        if length % rows == 0:
            return rows
    return length


def vmem(count):
    return [pl.BlockSpec(memory_space=pltpu.VMEM)] * count


def params(**more):
    return pltpu.CompilerParams(vmem_limit_bytes=VMEM_BYTES, **more)


def anywhere(count):
    return [pl.BlockSpec(memory_space=pl.ANY)] * count


def remote(src, dst, sems, index, axis, peer):
    return pltpu.make_async_remote_copy(
        src_ref=src,
        dst_ref=dst,
        send_sem=sems.at[0, index],
        recv_sem=sems.at[1, index],
        device_id={axis: peer},
        device_id_type=pl.DeviceIdType.MESH,
    )


def narrow_mates():
    me = lax.axis_index("narrow")
    row, core = me // 2, me % 2
    return me, row, core, (1 - row) * 2 + core, row * 2 + 1 - core


def greet(wide_peers=0):
    _, _, _, over, beside = narrow_mates()
    barrier = pltpu.get_barrier_semaphore()
    mesh_id = pl.DeviceIdType.MESH
    pl.semaphore_signal(barrier, inc=1, device_id={"narrow": over}, device_id_type=mesh_id)
    pl.semaphore_signal(barrier, inc=1, device_id={"narrow": beside}, device_id_type=mesh_id)
    if wide_peers:
        place = lax.axis_index("wide")
        _, row, core, _, _ = narrow_mates()
        pl.semaphore_signal(
            barrier, inc=1, device_id={"narrow": (1 - row) * 2 + 1 - core}, device_id_type=mesh_id
        )
        for step in range(1, wide_peers):
            peer = lax.rem(place + step, wide_peers)
            pl.semaphore_signal(barrier, inc=1, device_id={"wide": peer}, device_id_type=mesh_id)
    pl.semaphore_wait(barrier, 2 + (wide_peers if wide_peers else 0))


def norm_parts(values):
    center = values - jnp.mean(values, axis=-1, keepdims=True)
    spread = jnp.mean(center * center, axis=-1, keepdims=True)
    inverse = lax.rsqrt(spread + layer_eps)
    return center * inverse, inverse


def norm_back(xhat, inverse, gain, grad):
    scaled = gain * grad
    mean_one = jnp.mean(scaled, axis=-1, keepdims=True)
    mean_two = jnp.mean(scaled * xhat, axis=-1, keepdims=True)
    return inverse * (scaled - mean_one - xhat * mean_two)


def row_sums(values):
    return jnp.sum(values.reshape(-1, 8, values.shape[-1]), axis=0)


def block_of(step, width=BLK):
    return pl.ds(pl.multiple_of(step * width, width), width)


def attention_block(length, shifted, pair, here, q_t, k_nat, v_t, out_t, lse, probs, qbd):
    rows = key_chunk(length)
    low = pair * PAIR
    qbd[0:HEAD_DIM, 0:BLK] = q_t[low : low + HEAD_DIM, here]
    qbd[HEAD_DIM:PAIR, BLK:WIDE_COLS] = q_t[low + HEAD_DIM : low + PAIR, here]
    queries = qbd[...]

    def scores(start):
        return dot(k_nat[start : start + rows, low : low + PAIR], queries) * SCORE

    top = jnp.zeros((1, WIDE_COLS), f32)
    if shifted:
        top = jnp.full((1, WIDE_COLS), -jnp.inf, f32)
        for start in range(0, length, rows):
            top = jnp.maximum(top, jnp.max(scores(start), axis=0, keepdims=True))
    total = jnp.zeros((8, WIDE_COLS), f32)
    for start in range(0, length, rows):
        score = scores(start)
        weight = jnp.exp2(score - top) if shifted else jnp.exp2(score)
        total = total + row_sums(weight)
        probs[start : start + rows, 0:WIDE_COLS] = weight.astype(bf16)
    total = jnp.sum(total, axis=0, keepdims=True)
    mixed = dot(v_t[low : low + PAIR, :], probs[:, 0:WIDE_COLS]) / total
    out_t[low : low + HEAD_DIM, here] = mixed[0:HEAD_DIM, 0:BLK]
    out_t[low + HEAD_DIM : low + PAIR, here] = mixed[HEAD_DIM:PAIR, BLK:WIDE_COLS]
    log_total = top + jnp.log2(total)
    lse[2 * pair : 2 * pair + 1, here] = log_total[:, 0:BLK]
    lse[2 * pair + 1 : 2 * pair + 2, here] = log_total[:, BLK:WIDE_COLS]


def front_kernel(
    length,
    tok,
    own_in,
    own_out,
    own_up,
    own_down,
    npar,
    w_in_out,
    w_out,
    w_up,
    w_down,
    x1,
    k_nat,
    v_nat,
    q_nat,
    q_t,
    k_t,
    v_t,
    out_t,
    lse,
    xbuf,
    probs,
    qbd,
    w_in,
    low_out,
    low_up,
    low_down,
    sem,
    own_sem,
    over_sem,
    beside_sem,
    pass_sem,
):
    padded = x1.shape[0]
    blocks = padded // BLK
    me, _, _, over, beside = narrow_mates()
    copy = pltpu.make_async_copy(tok.at[me], xbuf.at[pl.ds(0, length)], sem)
    copy.start()

    def slot(index, who):
        if index == 0:
            return w_in.at[:, pl.ds(pl.multiple_of(who * HEAD_DIM, HEAD_DIM), HEAD_DIM), :]
        if index == 1:
            return w_out.at[pl.ds(pl.multiple_of(who * HEAD_DIM, HEAD_DIM), HEAD_DIM), :]
        if index == 2:
            return w_up.at[:, pl.ds(pl.multiple_of(who * D, D), D)]
        return w_down.at[pl.ds(pl.multiple_of(who * D, D), D), :]

    def source(index):
        return (slot(0, me), low_out, low_up, low_down)[index]

    for which in range(3):
        w_in[which, pl.ds(pl.multiple_of(me * HEAD_DIM, HEAD_DIM), HEAD_DIM), :] = own_in[which].astype(bf16)
    low_out[...] = own_out[...].astype(bf16)
    low_up[...] = own_up[...].astype(bf16)
    low_down[...] = own_down[...].astype(bf16)
    greet()
    to_over = [remote(source(k), slot(k, me), over_sem, k, "narrow", over) for k in range(4)]
    to_beside = [remote(source(k), slot(k, me), beside_sem, k, "narrow", beside) for k in range(4)]
    passed = [remote(slot(k, over), slot(k, over), pass_sem, k, "narrow", beside) for k in range(4)]
    mine = [pltpu.make_async_copy(source(k), slot(k, me), own_sem.at[k]) for k in range(1, 4)]
    to_over[0].start()
    to_beside[0].start()

    if padded > length:
        xbuf[length:, :] = jnp.zeros((padded - length, D), bf16)
        probs[length:, :] = jnp.zeros((padded - length, WIDE_COLS), bf16)
    qbd[...] = jnp.zeros(qbd.shape, bf16)
    lse[...] = jnp.zeros(lse.shape, f32)
    copy.wait()
    gain = npar[0:1, :]
    shift = npar[1:2, :]

    @pl.loop(0, blocks)
    def norm(step):
        here = block_of(step)
        xhat, _ = norm_parts(xbuf[here, :].astype(f32))
        x1[here, :] = (xhat * gain + shift).astype(bf16)

    to_over[0].wait_recv()
    passed[0].start()
    for k in range(1, 4):
        to_over[k].start()
        to_beside[k].start()
        mine[k - 1].start()
    to_beside[0].wait_recv()
    passed[0].wait_recv()

    @pl.loop(0, blocks)
    def project(step):
        here = block_of(step)
        act = x1[here, :]
        q_nat[here, :] = dot(act, w_in[0], NT).astype(bf16)
        k_nat[here, :] = dot(act, w_in[1], NT).astype(bf16)
        v_nat[here, :] = dot(act, w_in[2], NT).astype(bf16)
        q_t[:, here] = dot(w_in[0], act, NT).astype(bf16)
        k_t[:, here] = dot(w_in[1], act, NT).astype(bf16)
        v_t[:, here] = dot(w_in[2], act, NT).astype(bf16)

    w_in_out[...] = w_in[...]
    if padded > length:
        v_t[:, length:] = jnp.zeros((D, padded - length), bf16)

    for pair in range(HEADS // 2):

        @pl.loop(0, blocks)
        def block(step):
            attention_block(length, False, pair, block_of(step), q_t, k_nat, v_t, out_t, lse, probs, qbd)

        if pair == 0:
            for k in range(1, 4):
                to_over[k].wait_recv()
                passed[k].start()

    for k in range(1, 4):
        to_beside[k].wait_recv()
        passed[k].wait_recv()
        mine[k - 1].wait()
    for k in range(4):
        to_over[k].wait_send()
        to_beside[k].wait_send()
        passed[k].wait_send()


def front(tokens, own_in, own_out, own_up, own_down, npar):
    length = tokens.shape[1]
    padded = ceil_to(length, BLK)
    shape = jax.ShapeDtypeStruct
    return pl.pallas_call(
        functools.partial(front_kernel, length),
        out_shape=(
            shape((3, D, D), bf16),
            shape((D, D), bf16),
            shape((D, FF), bf16),
            shape((FF, D), bf16),
            shape((padded, D), bf16),
            shape((padded, D), bf16),
            shape((padded, D), bf16),
            shape((padded, D), bf16),
            shape((D, padded), bf16),
            shape((D, padded), bf16),
            shape((D, padded), bf16),
            shape((D, padded), f32),
            shape((8, padded), f32),
        ),
        in_specs=anywhere(1) + vmem(5),
        out_specs=tuple(vmem(1) + anywhere(3) + vmem(9)),
        scratch_shapes=[
            pltpu.VMEM((padded, D), bf16),
            pltpu.VMEM((padded, WIDE_COLS), bf16),
            pltpu.VMEM((PAIR, WIDE_COLS), bf16),
            pltpu.VMEM((3, D, D), bf16),
            pltpu.VMEM(own_out.shape, bf16),
            pltpu.VMEM(own_up.shape, bf16),
            pltpu.VMEM(own_down.shape, bf16),
            pltpu.SemaphoreType.DMA,
            pltpu.SemaphoreType.DMA((4,)),
            pltpu.SemaphoreType.DMA((2, 4)),
            pltpu.SemaphoreType.DMA((2, 4)),
            pltpu.SemaphoreType.DMA((2, 4)),
        ],
        compiler_params=params(collective_id=1, has_side_effects=True),
        name="front",
    )(tokens, own_in, own_out, own_up, own_down, npar)


def shared_rows(rows, wide):
    return ceil_to(-(-rows // wide), 16) * wide


def early_rows(wide):
    return shared_rows(2 * D + HEAD_DIM, wide)


def late_rows(wide):
    return shared_rows(3 * HEAD_DIM + 8, wide)


def softplus(values):
    return jnp.maximum(values, 0.0) + jnp.log1p(jnp.exp(-jnp.abs(values)))


def sigmoid(values):
    return 1.0 / (1.0 + jnp.exp(-values))


def head_grads(logits, counts, library, genes, length):
    lane = lax.broadcasted_iota(jnp.int32, logits[0].shape, 1)
    valid = (lane >= CLASS_TOK) & (lane < length)
    mean_logit = jnp.where(valid, logits[0], -jnp.inf)
    top = jnp.max(mean_logit, axis=1, keepdims=True)
    raised = jnp.exp(mean_logit - top)
    total = jnp.sum(raised, axis=1, keepdims=True)
    share = raised / total
    log_mean = jnp.where(valid, logits[0], 0.0) - top - jnp.log(total) + jnp.log(library)
    disp = 0.5 + softplus(logits[1])
    log_disp = jnp.log(disp)
    inflate = logits[2]
    gap = log_mean - log_disp
    mean_part = sigmoid(gap)
    disp_part = sigmoid(-gap)
    log_both = jnp.maximum(log_disp, log_mean) + jnp.log1p(jnp.exp(-jnp.abs(gap)))
    shared = disp * (log_disp - log_both)
    shared_disp = (log_disp - log_both) + mean_part
    shared_mean = -disp * mean_part
    none = counts == 0.0
    lean = sigmoid(shared - inflate)
    psi = jnp.zeros_like(disp)
    for step in range(7):
        psi = psi + jnp.where(counts > step, 1.0 / (disp + step), 0.0)
    grad_disp = jnp.where(none, -lean * shared_disp, counts * disp_part / disp - shared_disp - psi)
    grad_mean = jnp.where(none, -lean * shared_mean, -shared_mean - counts * disp_part)
    grad_inflate = jnp.where(none, lean - sigmoid(-inflate), sigmoid(inflate))
    part = 1.0 / genes
    grad_disp = jnp.where(valid, grad_disp * part, 0.0)
    grad_mean = jnp.where(valid, grad_mean * part, 0.0)
    grad_inflate = jnp.where(valid, grad_inflate * part, 0.0)
    grad_zero = grad_mean - share * jnp.sum(grad_mean, axis=1, keepdims=True)
    return (grad_zero, grad_disp * sigmoid(logits[1]), grad_inflate)


def middle_kernel(
    length,
    tok,
    first_out_t,
    first_lse,
    q_t,
    k_nat,
    v_t,
    w_out,
    w_up,
    w_down,
    npar,
    head,
    counts,
    library,
    output,
    grad_mid,
    g_nat,
    g_t,
    delta,
    lse,
    early,
    grad_norm,
    grad_head,
    xbuf,
    out_t,
    mixed_t,
    mid,
    res,
    act,
    hidden,
    slope,
    res_low,
    grad_before,
    mid_low,
    logits,
    qbd,
    sem,
    out_sem,
):
    padded = xbuf.shape[0]
    blocks = padded // BLK
    me = lax.axis_index("narrow")
    copy = pltpu.make_async_copy(tok.at[me], xbuf.at[pl.ds(0, length)], sem)
    copy.start()
    get_out = pltpu.make_async_copy(first_out_t, out_t, out_sem)
    get_out.start()
    if padded > length:
        xbuf[length:, :] = jnp.zeros((padded - length, D), bf16)
    grad_norm[...] = jnp.zeros(grad_norm.shape, f32)
    grad_head[...] = jnp.zeros(grad_head.shape, f32)
    copy.wait()
    get_out.wait()
    gain = npar[2:3, :]
    shift = npar[3:4, :]

    level = first_lse[...]
    lse[...] = level
    good = (level > -80.0) & (level < 120.0)
    wrong = jnp.max(jnp.where(good, 0.0, 1.0))

    @pl.when(wrong > 0.0)
    def again():
        queries, keys, values = mixed_t, grad_before.at[:, 0:D], g_t
        for src, dst in ((q_t, queries), (k_nat, keys), (v_t, values)):
            fetch = pltpu.make_async_copy(src, dst, out_sem)
            fetch.start()
            fetch.wait()
        if padded > length:
            hidden[length:, 0:WIDE_COLS] = jnp.zeros((padded - length, WIDE_COLS), bf16)
        qbd[...] = jnp.zeros(qbd.shape, bf16)
        for pair in range(HEADS // 2):

            @pl.loop(0, blocks)
            def block(step):
                attention_block(length, True, pair, block_of(step), queries, keys, values, out_t, lse, hidden, qbd)

    @pl.loop(0, blocks)
    def forward(step):
        here = block_of(step)
        mixed = out_t[:, here].astype(bf16)
        mixed_t[:, here] = mixed
        middle = xbuf[here, :].astype(f32) + dot(mixed, w_out[...], TN)
        mid[here, :] = middle
        xhat, _ = norm_parts(middle)
        low = (xhat * gain + shift).astype(bf16)
        act[here, :] = low
        before = dot(low, w_up[...])
        square = before * before
        bend = jnp.tanh(GELU_A * before * (1.0 + GELU_B * square))
        half = 0.5 + 0.5 * bend
        hid = (before * half).astype(bf16)
        hidden[here, :] = hid
        slope[here, :] = half + 0.5 * before * (1.0 - bend * bend) * (GELU_A + 3.0 * GELU_A * GELU_B * square)
        result = middle + dot(hid, w_down[...])
        res[here, :] = result
        logits[:, here] = dot(head[...], result, NT, HI)

    output[...] = res[0:length, :].astype(bf16)
    genes = length - CLASS_TOK
    zero, disp, inflate = head_grads(
        (logits[0:1, :], logits[1:2, :], logits[2:3, :]),
        counts[0:1, :].astype(f32),
        library[0:1, 0:1].astype(f32),
        genes,
        length,
    )
    logits[0:1, :] = zero
    logits[1:2, :] = disp
    logits[2:3, :] = inflate
    logits[3:8, :] = jnp.zeros((5, padded), f32)

    @pl.loop(0, blocks)
    def backward(step):
        here = block_of(step)
        down_logits = logits[:, here]
        grad_res = dot(down_logits, head[...], TN, HI)
        grad_head[...] += dot(down_logits, res[here, :], NN, HI)
        low = grad_res.astype(bf16)
        res_low[here, :] = low
        grad_hidden = dot(low, w_down[...], NT)
        back = (slope[here, :] * grad_hidden).astype(bf16)
        grad_before[here, :] = back
        grad_two = dot(back, w_up[...], NT)
        xhat, inverse = norm_parts(mid[here, :])
        grad_norm[0:8, :] += row_sums(grad_two * xhat)
        grad_norm[8:16, :] += row_sums(grad_two)
        total = grad_res + norm_back(xhat, inverse, gain, grad_two)
        mid[here, :] = total
        total_low = total.astype(bf16)
        mid_low[here, :] = total_low
        g_nat[here, :] = dot(total_low, w_out[...], NT).astype(bf16)
        grad_t = dot(w_out[...], total_low, NT).astype(bf16)
        g_t[:, here] = grad_t
        inner = grad_t.astype(f32) * out_t[:, here]
        delta[:, here] = jnp.concatenate(
            [
                jnp.sum(inner[h * HEAD_DIM : (h + 1) * HEAD_DIM], axis=0, keepdims=True)
                for h in range(HEADS)
            ]
            + [jnp.zeros((8 - HEADS, BLK), f32)],
            axis=0,
        )

    grad_mid[...] = mid[...]
    grad_down = dot(res_low[...], hidden[...], TN)
    grad_up = dot(act[...], grad_before[...], TN)
    grad_out = dot(mixed_t[...], mid_low[...])
    used = 2 * D + HEAD_DIM
    for who in range(HEADS):
        part = early.at[who % 2, who // 2]
        part[0:D, :] = grad_down[:, who * D : (who + 1) * D]
        part[D : 2 * D, :] = grad_up[:, who * D : (who + 1) * D]
        part[2 * D : used, :] = grad_out[who * HEAD_DIM : (who + 1) * HEAD_DIM, :]
        if early.shape[2] > used:
            part[used:, :] = jnp.zeros((early.shape[2] - used, D), f32)


def middle_stage(wide, tokens, out_t, lse, q_t, k_nat, v_t, w_out, w_up, w_down, npar, head, counts, library):
    length = tokens.shape[1]
    padded = out_t.shape[1]
    shape = jax.ShapeDtypeStruct
    return pl.pallas_call(
        functools.partial(middle_kernel, length),
        out_shape=(
            shape((length, D), bf16),
            shape((padded, D), f32),
            shape((padded, D), bf16),
            shape((D, padded), bf16),
            shape((8, padded), f32),
            shape((8, padded), f32),
            shape((2, 2, early_rows(wide), D), f32),
            shape((16, D), f32),
            shape((8, D), f32),
        ),
        in_specs=anywhere(2) + vmem(1) + anywhere(3) + vmem(7),
        out_specs=tuple(vmem(9)),
        scratch_shapes=[
            pltpu.VMEM((padded, D), bf16),
            pltpu.VMEM((D, padded), f32),
            pltpu.VMEM((D, padded), bf16),
            pltpu.VMEM((padded, D), f32),
            pltpu.VMEM((padded, D), f32),
            pltpu.VMEM((padded, D), bf16),
            pltpu.VMEM((padded, FF), bf16),
            pltpu.VMEM((padded, FF), f32),
            pltpu.VMEM((padded, D), bf16),
            pltpu.VMEM((padded, FF), bf16),
            pltpu.VMEM((padded, D), bf16),
            pltpu.VMEM((8, padded), f32),
            pltpu.VMEM((PAIR, WIDE_COLS), bf16),
            pltpu.SemaphoreType.DMA,
            pltpu.SemaphoreType.DMA,
        ],
        compiler_params=params(),
        name="middle",
    )(tokens, out_t, lse, q_t, k_nat, v_t, w_out, w_up, w_down, npar, head, counts, library)


class Shares:
    def __init__(self, stack, bufs, sems, wide):
        self.stack = stack
        self.held, self.got, self.keep, self.send, self.come, self.parts, self.arrived, self.total = bufs
        self.sems, self.wide = sems, wide
        self.me, self.row, self.core, self.over, self.beside = narrow_mates()
        self.place = lax.axis_index("wide")

    def peer(self, step):
        return lax.rem(self.place + step, self.wide)

    def to_beside(self):
        return remote(self.stack.at[1 - self.core], self.got, self.sems, 0, "narrow", self.beside)

    def to_over(self):
        return remote(self.send, self.come, self.sems, 1, "narrow", self.over)

    def spread(self, step):
        peer = self.peer(step)
        return remote(
            self.parts.at[peer], self.arrived.at[self.place], self.sems, 1 + step, "wide", peer
        )

    def share(self, step):
        peer = self.peer(step)
        mine = self.total.at[self.place]
        return remote(mine, mine, self.sems, self.wide + step, "wide", peer)

    def start_beside(self):
        self.to_beside().start()

    def start_over(self):
        copy = self.to_beside()
        copy.wait_recv()
        self.send[...] = (self.held[1 - self.row] + self.got[1 - self.row]).astype(bf16)
        self.to_over().start()
        self.keep[...] = self.held[self.row] + self.got[self.row]

    def start_spread(self):
        self.to_over().wait_recv()
        whole = (self.keep[...] + self.come[...].astype(f32)).astype(bf16)
        self.parts[...] = whole.reshape(self.parts.shape)
        for step in range(1, self.wide):
            self.spread(step).start()
        self.arrived[self.place] = self.parts[self.place]

    def start_share(self):
        for step in range(1, self.wide):
            self.spread(step).wait_recv()
        self.total[self.place] = jnp.sum(self.arrived[...].astype(f32), axis=0).astype(bf16)
        for step in range(1, self.wide):
            self.share(step).start()

    def finish(self):
        for step in range(1, self.wide):
            self.share(step).wait_recv()

    def settle(self):
        self.to_beside().wait_send()
        self.to_over().wait_send()
        for step in range(1, self.wide):
            self.spread(step).wait_send()
            self.share(step).wait_send()


def share_scratch(rows, wide, held):
    own = [pltpu.VMEM((2, rows, D), f32)] if held else []
    return own + [
        pltpu.VMEM((2, rows, D), f32),
        pltpu.VMEM((rows, D), f32),
        pltpu.VMEM((rows, D), bf16),
        pltpu.VMEM((rows, D), bf16),
        pltpu.VMEM((wide, rows // wide, D), bf16),
        pltpu.VMEM((wide, rows // wide, D), bf16),
        pltpu.VMEM((wide, rows // wide, D), bf16),
        pltpu.SemaphoreType.DMA((2, 2 * wide)),
    ]


def back_kernel(length, wide, *refs):
    tok, out_own, early = refs[0:3]
    x1, k_nat, v_nat, q_nat, q_t, k_t, g_nat, g_t, lse, delta, grad_mid, w_in, npar, norm_two, head_two = refs[3:18]
    out_all, grad_all, early_sum, late_sum, squares_out = refs[18:23]
    refs = refs[23:]
    xbuf, probs, dscore, qbd, gbd, qnd, gnd, dk, dv, dq_t, joined, grad_low, norm_one, late, squares = refs[0:15]
    sem, own_sems, out_sems, over_sems, beside_sems, pass_sems, square_sems = refs[15:22]
    early_bufs = refs[22:30]
    early_sems = refs[30]
    late_bufs = refs[31:38]
    late_sems = refs[38]

    padded = x1.shape[0]
    blocks = padded // BLK
    rows = key_chunk(length)
    chunks = length // rows
    me, row, core, over, beside = narrow_mates()
    copy = pltpu.make_async_copy(tok.at[me], xbuf.at[pl.ds(0, length)], sem)
    copy.start()
    hold = pltpu.make_async_copy(early.at[core], early_bufs[0], own_sems.at[0])
    hold.start()
    keep_out = pltpu.make_async_copy(out_own, out_all.at[me], own_sems.at[1])
    keep_out.start()
    greet(wide)
    first = Shares(early, early_bufs, early_sems, wide)
    last = Shares(late, (late.at[core],) + tuple(late_bufs), late_sems, wide)
    out_over = remote(out_own, out_all.at[me], out_sems, 0, "narrow", over)
    out_beside = remote(out_own, out_all.at[me], out_sems, 1, "narrow", beside)
    out_pass = remote(out_all.at[over], out_all.at[over], out_sems, 2, "narrow", beside)
    first.start_beside()
    out_over.start()
    out_beside.start()

    if padded > length:
        xbuf[length:, :] = jnp.zeros((padded - length, D), bf16)
        dscore[length:, :] = jnp.zeros((padded - length, WIDE_COLS), bf16)
        joined[1, length:, :] = jnp.zeros((padded - length, D), bf16)
        joined[2, length:, :] = jnp.zeros((padded - length, D), bf16)
    for ref in (qbd, gbd, qnd, gnd):
        ref[...] = jnp.zeros(ref.shape, bf16)
    norm_one[...] = jnp.zeros(norm_one.shape, f32)
    scale = HEAD_DIM ** (-0.5)

    def begin():
        hold.wait()
        first.start_over()

    def hand_on():
        out_over.wait_recv()
        out_pass.start()

    last_step = blocks - 1
    events = {
        (0, min(1, last_step)): begin,
        (0, min(5, last_step)): first.start_spread,
        (0, last_step): first.start_share,
        (1, min(4, last_step)): first.finish,
        (1, last_step): hand_on,
    }

    for pair in range(HEADS // 2):
        low = pair * PAIR
        mid = low + HEAD_DIM
        top = low + PAIR
        dk[...] = jnp.zeros(dk.shape, f32)
        dv[...] = jnp.zeros(dv.shape, f32)

        @pl.loop(0, blocks)
        def block(step):
            here = block_of(step)
            for (which, when), event in events.items():
                if which == pair:
                    pl.when(step == when)(event)
            qbd[0:HEAD_DIM, 0:BLK] = q_t[low:mid, here]
            qbd[HEAD_DIM:PAIR, BLK:WIDE_COLS] = q_t[mid:top, here]
            gbd[0:HEAD_DIM, 0:BLK] = g_t[low:mid, here]
            gbd[HEAD_DIM:PAIR, BLK:WIDE_COLS] = g_t[mid:top, here]
            both = q_nat[here, low:top]
            qnd[0:BLK, 0:HEAD_DIM] = both[:, 0:HEAD_DIM]
            qnd[BLK:WIDE_COLS, HEAD_DIM:PAIR] = both[:, HEAD_DIM:PAIR]
            both = g_nat[here, low:top]
            gnd[0:BLK, 0:HEAD_DIM] = both[:, 0:HEAD_DIM]
            gnd[BLK:WIDE_COLS, HEAD_DIM:PAIR] = both[:, HEAD_DIM:PAIR]
            queries = qbd[...]
            grads = gbd[...]
            level = jnp.concatenate([lse[2 * pair : 2 * pair + 1, here], lse[2 * pair + 1 : 2 * pair + 2, here]], axis=1)
            inner = jnp.concatenate(
                [delta[2 * pair : 2 * pair + 1, here], delta[2 * pair + 1 : 2 * pair + 2, here]], axis=1
            )
            for start in range(0, length, rows):
                part = slice(start, start + rows)
                weight = jnp.exp2(dot(k_nat[part, low:top], queries) * SCORE - level)
                probs[part, :] = weight.astype(bf16)
                change = dot(v_nat[part, low:top], grads) - inner
                dscore[part, :] = (weight * change).astype(bf16)
            dv[...] += dot(probs[...], gnd[...])
            dk[...] += dot(dscore[0:length, :], qnd[...])
            moved = dot(k_t[low:top, :], dscore[...]) * scale
            dq_t[low:mid, here] = moved[0:HEAD_DIM, 0:BLK].astype(bf16)
            dq_t[mid:top, here] = moved[HEAD_DIM:PAIR, BLK:WIDE_COLS].astype(bf16)

        joined[1, 0:length, low:top] = (dk[...] * scale).astype(bf16)
        joined[2, 0:length, low:top] = dv[...].astype(bf16)

    copy.wait()
    gain = npar[0:1, :]

    def close(step):
        here = block_of(step)
        grad_q = dq_t[:, here].T
        joined[0, here, :] = grad_q
        total = dot(grad_q, w_in[0]) + dot(joined[1, here, :], w_in[1]) + dot(joined[2, here, :], w_in[2])
        xhat, inverse = norm_parts(xbuf[here, :].astype(f32))
        norm_one[0:8, :] += row_sums(total * xhat)
        norm_one[8:16, :] += row_sums(total)
        grad_low[here, :] = (grad_mid[here, :] + norm_back(xhat, inverse, gain, total)).astype(bf16)

    def chunk(index, who):
        return grad_all.at[who, pl.ds(index * rows, rows)]

    def held(index):
        return grad_low.at[pl.ds(index * rows, rows)]

    to_over = [remote(held(k), chunk(k, me), over_sems, k, "narrow", over) for k in range(chunks)]
    to_beside = [remote(held(k), chunk(k, me), beside_sems, k, "narrow", beside) for k in range(chunks)]
    passed = [remote(chunk(k, over), chunk(k, over), pass_sems, k, "narrow", beside) for k in range(chunks)]
    mine = pltpu.make_async_copy(grad_low.at[pl.ds(0, length)], grad_all.at[me], own_sems.at[2])

    half = -(-blocks // 2)
    ready = half * BLK // rows
    pl.loop(0, half)(close)
    for k in range(ready):
        to_over[k].start()
    pl.loop(half, blocks)(close)
    mine.start()
    for k in range(chunks):
        to_beside[k].start()

    late[...] = jnp.zeros(late.shape, f32)
    for which in range(3):
        grad_w = dot(joined[which], x1[...], TN)
        for who in range(HEADS):
            late[who % 2, who // 2, which * HEAD_DIM : (which + 1) * HEAD_DIM, :] = grad_w[
                who * HEAD_DIM : (who + 1) * HEAD_DIM, :
            ]
    sums = [norm_one[0:8, :], norm_one[8:16, :], norm_two[0:8, :], norm_two[8:16, :]]
    extra = jnp.concatenate([jnp.sum(v, axis=0, keepdims=True) for v in sums] + [head_two[0:4, :]], axis=0)
    for who in range(HEADS):
        late[who % 2, who // 2, 3 * HEAD_DIM : 3 * HEAD_DIM + 8, :] = extra
    last.start_beside()
    early_sum[...] = first.total[...].reshape(early_sum.shape)
    last.start_over()
    last.start_spread()
    for k in range(ready, chunks):
        to_over[k].start()
    last.start_share()
    for k in range(ready):
        to_over[k].wait_recv()
        passed[k].start()
    last.finish()
    late_sum[...] = last.total[...].reshape(late_sum.shape)
    whole = early_sum[...].astype(f32)
    part = late_sum[0 : 3 * HEAD_DIM, :].astype(f32)
    level = jnp.sum(row_sums(whole * whole) + row_sums(part * part), axis=(0, 1), keepdims=True)
    squares[me] = jnp.broadcast_to(level, squares.shape[1:])
    told = []
    for index, mate in enumerate((over, beside, (1 - row) * 2 + 1 - core)):
        tell = remote(squares.at[me], squares.at[me], square_sems, index, "narrow", mate)
        tell.start()
        told.append(tell)
    for k in range(ready, chunks):
        to_over[k].wait_recv()
        passed[k].start()
    for tell in told:
        tell.wait_recv()
    squares_out[...] = squares[...]
    keep_out.wait()
    mine.wait()
    out_beside.wait_recv()
    out_pass.wait_recv()
    for k in range(chunks):
        to_beside[k].wait_recv()
        passed[k].wait_recv()
    for tell in told + [out_over, out_beside, out_pass] + to_over + to_beside + passed:
        tell.wait_send()
    first.settle()
    last.settle()


def back_stage(wide, tokens, out_own, early, *rest):
    cells, length, _ = tokens.shape
    padded = rest[0].shape[0]
    chunks = length // key_chunk(length)
    shape = jax.ShapeDtypeStruct
    return pl.pallas_call(
        functools.partial(back_kernel, length, wide),
        out_shape=(
            shape((cells, length, D), bf16),
            shape((cells, length, D), bf16),
            shape((early_rows(wide), D), bf16),
            shape((late_rows(wide), D), bf16),
            shape((HEADS, 8, 128), f32),
        ),
        in_specs=anywhere(3) + vmem(15),
        out_specs=tuple(anywhere(2) + vmem(3)),
        scratch_shapes=[
            pltpu.VMEM((padded, D), bf16),
            pltpu.VMEM((length, WIDE_COLS), bf16),
            pltpu.VMEM((padded, WIDE_COLS), bf16),
            pltpu.VMEM((PAIR, WIDE_COLS), bf16),
            pltpu.VMEM((PAIR, WIDE_COLS), bf16),
            pltpu.VMEM((WIDE_COLS, PAIR), bf16),
            pltpu.VMEM((WIDE_COLS, PAIR), bf16),
            pltpu.VMEM((length, PAIR), f32),
            pltpu.VMEM((length, PAIR), f32),
            pltpu.VMEM((D, padded), bf16),
            pltpu.VMEM((3, padded, D), bf16),
            pltpu.VMEM((padded, D), bf16),
            pltpu.VMEM((16, D), f32),
            pltpu.VMEM((2, 2, late_rows(wide), D), f32),
            pltpu.VMEM((HEADS, 8, 128), f32),
            pltpu.SemaphoreType.DMA,
            pltpu.SemaphoreType.DMA((3,)),
            pltpu.SemaphoreType.DMA((2, 3)),
            pltpu.SemaphoreType.DMA((2, chunks)),
            pltpu.SemaphoreType.DMA((2, chunks)),
            pltpu.SemaphoreType.DMA((2, chunks)),
            pltpu.SemaphoreType.DMA((2, 3)),
        ]
        + share_scratch(early_rows(wide), wide, True)
        + share_scratch(late_rows(wide), wide, False),
        compiler_params=params(collective_id=2, has_side_effects=True),
        name="back",
    )(tokens, out_own, early, *rest)


def adam_update(grad, first, second, weight, decay_rate, rate):
    first_new = decay_first * first + (1.0 - decay_first) * grad
    second_new = decay_second * second + (1.0 - decay_second) * grad * grad
    fix_first = 1.0 - decay_first**STEP
    fix_second = 1.0 - decay_second**STEP
    direction = first_new / fix_first / (jnp.sqrt(second_new / fix_second) + adam_eps)
    return (first_new, second_new, weight - rate * (direction + decay_rate * weight))


def finish_kernel(early, late, squares, *refs):
    ins, outs = refs[0:24], refs[24:]
    grad_norm_ref, outs = outs[0], outs[1:]
    place = lax.axis_index("wide")
    whole = early[...].astype(f32)
    small = late[...].astype(f32)
    extra = small[3 * HEAD_DIM : 3 * HEAD_DIM + 8, :]
    live = lax.broadcasted_iota(jnp.int32, extra.shape, 0) < 7
    extra = jnp.where(live, extra, 0.0)
    shards = jnp.sum(squares[...], axis=0)[0:1, 0:1]
    grad_norm = jnp.sqrt(shards + jnp.sum(extra * extra, axis=(0, 1), keepdims=True))
    grad_norm_ref[...] = grad_norm
    factor = jnp.minimum(1.0, clip_limit / grad_norm)
    grads = (
        None,
        whole[2 * D : 2 * D + HEAD_DIM, :],
        whole[D : 2 * D, :],
        whole[0:D, :].T,
        extra[0:4, :],
        extra[4:7, :],
    )
    decays = (weight_decay,) * 4 + (0.0, weight_decay)
    rates = (learn_rate,) * 4 + (norm_rate, learn_rate)

    def update(index, grad, at):
        weight, first, second = ins[index][at], ins[6 + index][at], ins[12 + index][at]
        clipped = grad * factor
        first_new, second_new, weight_new = adam_update(clipped, first, second, weight, decays[index], rates[index])
        outs[5 * index][at] = clipped
        outs[5 * index + 1][at] = first_new
        outs[5 * index + 2][at] = second_new
        outs[5 * index + 3][at] = weight_new
        return weight_new

    def mean(index, at, piece):
        outs[5 * index + 4][at] = ema_keep * ins[18 + index][at] + (1.0 - ema_keep) * piece

    def rows_here(values, count):
        return pltpu.roll(values, lax.rem(D - place * count, D), 0)[0:count, :]

    for which in range(3):
        weight_new = update(0, small[which * HEAD_DIM : (which + 1) * HEAD_DIM, :], which)
        mean(0, which, rows_here(weight_new.T, ins[18].shape[1]))
    for index in range(1, 4):
        weight_new = update(index, grads[index], Ellipsis)
        mean(index, Ellipsis, rows_here(weight_new if index == 2 else weight_new.T, ins[18 + index].shape[0]))
    for index in range(4, 6):
        weight_new = update(index, grads[index], Ellipsis)
        rows, count = ins[18 + index].shape
        full = jnp.concatenate([weight_new, jnp.zeros((8 - rows, D), f32)], axis=0)
        turned = pltpu.roll(full, lax.rem(D - place * count, D), 1)
        mean(index, Ellipsis, turned[0:rows, 0:count])


def finish(early, late, squares, state):
    shape = jax.ShapeDtypeStruct
    outs = [shape((1, 1), f32)]
    for index in range(6):
        outs += [shape(state[index].shape, f32)] * 4 + [shape(state[18 + index].shape, f32)]
    return pl.pallas_call(
        finish_kernel,
        out_shape=tuple(outs),
        in_specs=vmem(27),
        out_specs=tuple(vmem(31)),
        compiler_params=params(),
        name="finish",
    )(early, late, squares, *state)


def on_device(cell_tokens, library_size, gene_counts, *state):
    turn = lambda v: jnp.swapaxes(v, -1, -2)
    state = tuple(turn(v) if index in (0, 6, 12, 19, 21) else v for index, v in enumerate(state))
    attend_in, attend_out, up_weight, down_weight, norm_params, head_weight = state[0:6]
    cells, length, _ = cell_tokens.shape
    padded = ceil_to(length, BLK)
    me = lax.axis_index("narrow")
    wide = lax.axis_size("wide")
    head = jnp.pad(head_weight, ((0, 5), (0, 0)))
    counts = lax.dynamic_slice_in_dim(gene_counts, me, 1, 0)
    counts = jnp.pad(counts, ((0, 0), (CLASS_TOK, padded - length)))
    library = lax.dynamic_slice_in_dim(library_size, me, 1, 0).reshape(1, 1)

    w_in, w_out, w_up, w_down, x1, k_nat, v_nat, q_nat, q_t, k_t, v_t, out_t, lse = front(
        cell_tokens, attend_in, attend_out, up_weight, down_weight, norm_params
    )
    out_own, grad_mid, g_nat, g_t, delta, lse, early, norm_two, head_two = middle_stage(
        wide, cell_tokens, out_t, lse, q_t, k_nat, v_t, w_out, w_up, w_down, norm_params, head, counts, library
    )
    out_all, grad_all, early, late, squares = back_stage(
        wide,
        cell_tokens,
        out_own,
        early,
        x1,
        k_nat,
        v_nat,
        q_nat,
        q_t,
        k_t,
        g_nat,
        g_t,
        lse,
        delta,
        grad_mid,
        w_in,
        norm_params,
        norm_two,
        head_two,
    )
    grad_norm, *updates = finish(early, late, squares, state)
    updates = [turn(v) if index in (0, 1, 2, 3, 9, 19) else v for index, v in enumerate(updates)]
    return (out_all, grad_all.astype(f32), grad_norm.reshape(()), *updates)


def solution(mesh):
    by_in, by_rows, by_cols = P(None, None, "narrow"), P("narrow", None), P(None, "narrow")
    kinds = (by_in, by_rows, by_cols, by_rows, P(), P())
    means = (
        P(None, "wide", "narrow"),
        P("narrow", "wide"),
        P("wide", "narrow"),
        P("narrow", "wide"),
        P(None, "wide"),
        P(None, "wide"),
    )
    cell = P("wide", None, None)
    outs = (cell, cell, P())
    for kind, mean in zip(kinds, means):
        outs += (kind, kind, kind, kind, mean)
    return jax.shard_map(
        on_device,
        mesh=mesh,
        in_specs=(cell, P("wide"), P("wide", None)) + kinds * 3 + means,
        out_specs=outs,
        check_vma=False,
    )
```

```python
import functools

import jax
import jax.numpy as jnp
from jax import lax
from jax.experimental import pallas as pl
from jax.experimental.pallas import tpu as pltpu
from jax.sharding import PartitionSpec as P

D = 256
FF = 1024
HEADS = 4
HEAD_DIM = 64
CLASS_TOK = 8
STEP = 10

layer_eps = 1e-05
clip_limit = 0.25
decay_first = 0.9
decay_second = 0.999
learn_rate = 0.06
norm_rate = 0.6
adam_eps = 1e-08
weight_decay = 0.01
ema_keep = 0.75

f32 = jnp.float32
bf16 = jnp.bfloat16

NN = (((1,), (0,)), ((), ()))
NT = (((1,), (1,)), ((), ()))
TN = (((0,), (0,)), ((), ()))

BLK = 256
PAIR = 2 * HEAD_DIM
WIDE_COLS = 2 * BLK
LOG2E = 1.4426950408889634
SCORE = LOG2E * HEAD_DIM ** (-0.5)
GELU_A = 0.7978845608028654
GELU_B = 0.044715
GROUP = 3
VMEM_BYTES = 60 * 2**20


def dot(left, right, dims=NN, precision=None):
    return lax.dot_general(left, right, dims, precision=precision, preferred_element_type=f32)


def ceil_to(value, unit):
    return -(-value // unit) * unit


def key_chunk(length):
    for rows in (368, 464, 320, 592, 256, 224, 288, 208, 176, 128, 64, 48, 32, 16):
        if length % rows == 0:
            return rows
    return length


def vmem(count):
    return [pl.BlockSpec(memory_space=pltpu.VMEM)] * count


def params(**more):
    return pltpu.CompilerParams(vmem_limit_bytes=VMEM_BYTES, **more)


def anywhere(count):
    return [pl.BlockSpec(memory_space=pl.ANY)] * count


def remote(src, dst, sems, index, axis, peer):
    return pltpu.make_async_remote_copy(
        src_ref=src,
        dst_ref=dst,
        send_sem=sems.at[0, index],
        recv_sem=sems.at[1, index],
        device_id={axis: peer},
        device_id_type=pl.DeviceIdType.MESH,
    )


def narrow_mates():
    me = lax.axis_index("narrow")
    row, core = me // 2, me % 2
    return me, row, core, (1 - row) * 2 + core, row * 2 + 1 - core


def greet(wide_peers=0):
    _, _, _, over, beside = narrow_mates()
    barrier = pltpu.get_barrier_semaphore()
    mesh_id = pl.DeviceIdType.MESH
    pl.semaphore_signal(barrier, inc=1, device_id={"narrow": over}, device_id_type=mesh_id)
    pl.semaphore_signal(barrier, inc=1, device_id={"narrow": beside}, device_id_type=mesh_id)
    if wide_peers:
        place = lax.axis_index("wide")
        _, row, core, _, _ = narrow_mates()
        pl.semaphore_signal(
            barrier, inc=1, device_id={"narrow": (1 - row) * 2 + 1 - core}, device_id_type=mesh_id
        )
        for step in range(1, wide_peers):
            peer = lax.rem(place + step, wide_peers)
            pl.semaphore_signal(barrier, inc=1, device_id={"wide": peer}, device_id_type=mesh_id)
    pl.semaphore_wait(barrier, 2 + (wide_peers if wide_peers else 0))


def norm_parts(values):
    center = values - jnp.mean(values, axis=-1, keepdims=True)
    spread = jnp.mean(center * center, axis=-1, keepdims=True)
    inverse = lax.rsqrt(spread + layer_eps)
    return center * inverse, inverse


def norm_back(xhat, inverse, gain, grad):
    scaled = gain * grad
    mean_one = jnp.mean(scaled, axis=-1, keepdims=True)
    mean_two = jnp.mean(scaled * xhat, axis=-1, keepdims=True)
    return inverse * (scaled - mean_one - xhat * mean_two)


def row_sums(values):
    return jnp.sum(values.reshape(-1, 8, values.shape[-1]), axis=0)


def block_of(step, width=BLK):
    if isinstance(step, int):
        return pl.ds(step * width, width)
    return pl.ds(pl.multiple_of(step * width, width), width)


def attention_block(length, shifted, pair, here, q_t, k_nat, v_t, out_t, totals, probs, qbd):
    rows = key_chunk(length)
    low = pair * PAIR
    qbd[0:HEAD_DIM, 0:BLK] = q_t[low : low + HEAD_DIM, here]
    qbd[HEAD_DIM:PAIR, BLK:WIDE_COLS] = q_t[low + HEAD_DIM : low + PAIR, here]
    queries = qbd[...]

    def scores(start):
        return dot(k_nat[start : start + rows, low : low + PAIR], queries) * SCORE

    top = jnp.zeros((1, WIDE_COLS), f32)
    if shifted:
        top = jnp.full((1, WIDE_COLS), -jnp.inf, f32)
        for start in range(0, length, rows):
            top = jnp.maximum(top, jnp.max(scores(start), axis=0, keepdims=True))
    total = jnp.zeros((8, WIDE_COLS), f32)
    for start in range(0, length, rows):
        score = scores(start)
        weight = jnp.exp2(score - top) if shifted else jnp.exp2(score)
        total = total + row_sums(weight)
        probs[start : start + rows, 0:WIDE_COLS] = weight.astype(bf16)
    total = jnp.sum(total, axis=0, keepdims=True)
    mixed = dot(v_t[low : low + PAIR, :], probs[:, 0:WIDE_COLS]) / total
    out_t[low : low + HEAD_DIM, here] = mixed[0:HEAD_DIM, 0:BLK]
    out_t[low + HEAD_DIM : low + PAIR, here] = mixed[HEAD_DIM:PAIR, BLK:WIDE_COLS]
    totals[2 * pair : 2 * pair + 1, here] = total[:, 0:BLK]
    totals[2 * pair + 1 : 2 * pair + 2, here] = total[:, BLK:WIDE_COLS]


def front_kernel(
    length,
    tok,
    far_in,
    far_out,
    far_up,
    far_down,
    npar,
    w_out,
    w_up,
    w_down,
    *refs,
):
    weights, outs, refs = refs[0], refs[1:11], refs[11:]
    x1, k_nat, v_nat, q_nat, q_t, k_t, v_t, w_in, out_t, totals = refs[0:10]
    xbuf, probs, qbd, low_out, low_up, low_down, sem, own_sem, over_sem, beside_sem, pass_sem, save_sems = refs[10:22]
    weight_sems = refs[22]
    own_in, own_out, own_up, own_down = refs[23:27]
    padded = x1.shape[0]
    blocks = padded // BLK
    me, _, _, over, beside = narrow_mates()
    gets = save((far_in,), (own_in,), own_sem, 0)
    copy = pltpu.make_async_copy(tok.at[me], xbuf.at[pl.ds(0, length)], sem)
    copy.start()
    gets += save((far_out, far_up, far_down), (own_out, own_up, own_down), own_sem, 1)

    def slot(index, who):
        if index == 0:
            return w_in.at[:, pl.ds(pl.multiple_of(who * HEAD_DIM, HEAD_DIM), HEAD_DIM), :]
        if index == 1:
            return w_out.at[pl.ds(pl.multiple_of(who * HEAD_DIM, HEAD_DIM), HEAD_DIM), :]
        if index == 2:
            return w_up.at[:, pl.ds(pl.multiple_of(who * D, D), D)]
        return w_down.at[pl.ds(pl.multiple_of(who * D, D), D), :]

    def source(index):
        return (slot(0, me), low_out, low_up, low_down)[index]

    gets[0].wait()
    for which in range(3):
        w_in[which, pl.ds(pl.multiple_of(me * HEAD_DIM, HEAD_DIM), HEAD_DIM), :] = own_in[which].astype(bf16)
    greet()
    to_over = [remote(source(k), slot(k, me), over_sem, k, "narrow", over) for k in range(4)]
    to_beside = [remote(source(k), slot(k, me), beside_sem, k, "narrow", beside) for k in range(4)]
    passed = [remote(slot(k, over), slot(k, over), pass_sem, k, "narrow", beside) for k in range(4)]
    mine = [pltpu.make_async_copy(source(k), slot(k, me), own_sem.at[k]) for k in range(1, 4)]
    to_over[0].start()
    to_beside[0].start()
    for get in gets[1:]:
        get.wait()
    low_out[...] = own_out[...].astype(bf16)
    low_up[...] = own_up[...].astype(bf16)
    low_down[...] = own_down[...].astype(bf16)

    if padded > length:
        xbuf[length:, :] = jnp.zeros((padded - length, D), bf16)
        probs[:, :, length:, :] = jnp.zeros((2, HEADS // 2, padded - length, WIDE_COLS), bf16)
    qbd[...] = jnp.zeros(qbd.shape, bf16)
    totals[...] = jnp.ones(totals.shape, f32)
    copy.wait()
    gain = npar[0:1, :]
    shift = npar[1:2, :]

    @pl.loop(0, blocks)
    def norm(step):
        here = block_of(step)
        xhat, _ = norm_parts(xbuf[here, :].astype(f32))
        x1[here, :] = (xhat * gain + shift).astype(bf16)

    to_over[0].wait_recv()
    passed[0].start()
    for k in range(1, 4):
        to_over[k].start()
        to_beside[k].start()
        mine[k - 1].start()
    to_beside[0].wait_recv()
    passed[0].wait_recv()

    @pl.loop(0, blocks // GROUP)
    def project(step):
        here = block_of(step, GROUP * BLK)
        act = x1[here, :]
        q_nat[here, :] = dot(act, w_in[0], NT).astype(bf16)
        k_nat[here, :] = dot(act, w_in[1], NT).astype(bf16)
        v_nat[here, :] = dot(act, w_in[2], NT).astype(bf16)
        q_t[:, here] = dot(w_in[0], act, NT).astype(bf16)
        k_t[:, here] = dot(w_in[1], act, NT).astype(bf16)
        v_t[:, here] = dot(w_in[2], act, NT).astype(bf16)

    if padded > length:
        v_t[:, length:] = jnp.zeros((D, padded - length), bf16)

    half = (blocks // 2) * BLK

    def keep(step, pair, slot):
        return pltpu.make_async_copy(
            probs.at[slot, pair, pl.ds(0, length)], weights.at[step, pair], weight_sems.at[slot, pair]
        )

    def attend(step):
        here = block_of(step)
        slot = lax.rem(step, 2)

        @pl.when(step >= 2)
        def free():
            for pair in range(HEADS // 2):
                keep(step - 2, pair, slot).wait()

        for pair in range(HEADS // 2):
            attention_block(
                length, False, pair, here, q_t, k_nat, v_t, out_t, totals, probs.at[slot, pair], qbd.at[pair]
            )
            keep(step, pair, slot).start()

    saves = save((x1, k_nat, v_nat, q_nat, q_t, k_t, v_t, w_in), outs[0:8], save_sems, 0)
    pl.loop(0, blocks // 2)(attend)
    for k in range(1, 4):
        to_over[k].wait_recv()
        passed[k].start()
    saves += save((out_t.at[:, 0:half],), (outs[8].at[:, 0:half],), save_sems, 8)
    pl.loop(blocks // 2, blocks)(attend)
    saves += save((out_t.at[:, half:], totals), (outs[8].at[:, half:], outs[9]), save_sems, 9)
    for step in range(max(0, blocks - 2), blocks):
        for pair in range(HEADS // 2):
            keep(step, pair, step % 2).wait()
    for copy in saves:
        copy.wait()
    for k in range(1, 4):
        to_beside[k].wait_recv()
        passed[k].wait_recv()
        mine[k - 1].wait()
    for k in range(4):
        to_over[k].wait_send()
        to_beside[k].wait_send()
        passed[k].wait_send()


def save(sources, targets, sems, first):
    copies = [
        pltpu.make_async_copy(src, dst, sems.at[first + k]) for k, (src, dst) in enumerate(zip(sources, targets))
    ]
    for copy in copies:
        copy.start()
    return copies


def front(tokens, own_in, own_out, own_up, own_down, npar):
    length = tokens.shape[1]
    padded = ceil_to(length, BLK)
    shape = jax.ShapeDtypeStruct
    kept = (
        [((padded, D), bf16)] * 4
        + [((D, padded), bf16)] * 3
        + [((3, D, D), bf16), ((D, padded), f32), ((8, padded), f32)]
    )
    return pl.pallas_call(
        functools.partial(front_kernel, length),
        out_shape=tuple(
            [shape((D, D), bf16), shape((D, FF), bf16), shape((FF, D), bf16)]
            + [shape((padded // BLK, HEADS // 2, length, WIDE_COLS), bf16)]
            + [shape(*what) for what in kept]
        ),
        in_specs=anywhere(5) + vmem(1),
        out_specs=tuple(anywhere(14)),
        scratch_shapes=[pltpu.VMEM(*what) for what in kept]
        + [
            pltpu.VMEM((padded, D), bf16),
            pltpu.VMEM((2, HEADS // 2, padded, WIDE_COLS), bf16),
            pltpu.VMEM((HEADS // 2, PAIR, WIDE_COLS), bf16),
            pltpu.VMEM(own_out.shape, bf16),
            pltpu.VMEM(own_up.shape, bf16),
            pltpu.VMEM(own_down.shape, bf16),
            pltpu.SemaphoreType.DMA,
            pltpu.SemaphoreType.DMA((4,)),
            pltpu.SemaphoreType.DMA((2, 4)),
            pltpu.SemaphoreType.DMA((2, 4)),
            pltpu.SemaphoreType.DMA((2, 4)),
            pltpu.SemaphoreType.DMA((11,)),
            pltpu.SemaphoreType.DMA((2, HEADS // 2)),
            pltpu.VMEM(own_in.shape, f32),
            pltpu.VMEM(own_out.shape, f32),
            pltpu.VMEM(own_up.shape, f32),
            pltpu.VMEM(own_down.shape, f32),
        ],
        compiler_params=params(collective_id=1, has_side_effects=True),
        name="front",
    )(tokens, own_in, own_out, own_up, own_down, npar)


def shared_rows(rows, wide):
    return ceil_to(-(-rows // wide), 16) * wide


def early_rows(wide):
    return shared_rows(2 * D + HEAD_DIM, wide)


def late_rows(wide):
    return shared_rows(3 * HEAD_DIM + 16, wide)


def split(values):
    high = values.astype(bf16)
    return high, (values - high.astype(f32)).astype(bf16)


def softplus(values):
    return jnp.maximum(values, 0.0) + jnp.log1p(jnp.exp(-jnp.abs(values)))


def sigmoid(values):
    return 1.0 / (1.0 + jnp.exp(-values))


def head_grads(logits, counts, library, genes, length):
    lane = lax.broadcasted_iota(jnp.int32, logits[0].shape, 1)
    valid = (lane >= CLASS_TOK) & (lane < length)
    mean_logit = jnp.where(valid, logits[0], -jnp.inf)
    top = jnp.max(mean_logit, axis=1, keepdims=True)
    raised = jnp.exp(mean_logit - top)
    total = jnp.sum(raised, axis=1, keepdims=True)
    share = raised / total
    log_mean = jnp.where(valid, logits[0], 0.0) - top - jnp.log(total) + jnp.log(library)
    disp = 0.5 + softplus(logits[1])
    log_disp = jnp.log(disp)
    inflate = logits[2]
    gap = log_mean - log_disp
    mean_part = sigmoid(gap)
    disp_part = sigmoid(-gap)
    log_both = jnp.maximum(log_disp, log_mean) + jnp.log1p(jnp.exp(-jnp.abs(gap)))
    shared = disp * (log_disp - log_both)
    shared_disp = (log_disp - log_both) + mean_part
    shared_mean = -disp * mean_part
    none = counts == 0.0
    lean = sigmoid(shared - inflate)
    psi = jnp.zeros_like(disp)
    for step in range(7):
        psi = psi + jnp.where(counts > step, 1.0 / (disp + step), 0.0)
    grad_disp = jnp.where(none, -lean * shared_disp, counts * disp_part / disp - shared_disp - psi)
    grad_mean = jnp.where(none, -lean * shared_mean, -shared_mean - counts * disp_part)
    grad_inflate = jnp.where(none, lean - sigmoid(-inflate), sigmoid(inflate))
    part = 1.0 / genes
    grad_disp = jnp.where(valid, grad_disp * part, 0.0)
    grad_mean = jnp.where(valid, grad_mean * part, 0.0)
    grad_inflate = jnp.where(valid, grad_inflate * part, 0.0)
    grad_zero = grad_mean - share * jnp.sum(grad_mean, axis=1, keepdims=True)
    return (grad_zero, grad_disp * sigmoid(logits[1]), grad_inflate)


def middle_kernel(
    length,
    tok,
    first_out_t,
    first_totals,
    q_t,
    k_nat,
    v_t,
    weights,
    far_out,
    far_up,
    far_down,
    npar,
    head,
    counts,
    library,
    output,
    grad_mid,
    g_nat_out,
    g_t_out,
    early,
    weights_out,
    delta,
    inverse_totals,
    grad_norm,
    grad_head,
    xbuf,
    out_t,
    totals,
    g_nat,
    g_t,
    early_buf,
    mixed_t,
    mid,
    res_high,
    res_rest,
    act,
    hidden,
    slope,
    res_low,
    grad_before,
    mid_low,
    logits,
    downs,
    counted,
    qbd,
    w_out,
    w_up,
    w_down,
    sem,
    out_sem,
    send_sems,
):
    padded = xbuf.shape[0]
    blocks = padded // BLK
    me = lax.axis_index("narrow")
    copy = pltpu.make_async_copy(tok.at[me], xbuf.at[pl.ds(0, length)], sem)
    copy.start()
    get_out = pltpu.make_async_copy(first_out_t, out_t, out_sem)
    get_out.start()
    get_weights = save((far_out, far_up, far_down), (w_out, w_up, w_down), send_sems, 0)
    if padded > length:
        xbuf[length:, :] = jnp.zeros((padded - length, D), bf16)
    grad_norm[...] = jnp.zeros(grad_norm.shape, f32)
    copy.wait()
    get_out.wait()
    for get in get_weights:
        get.wait()
    gain = npar[2:3, :]
    shift = npar[3:4, :]

    level = first_totals[...]
    totals[...] = level
    good = (level > 1e-25) & (level < 1e36)
    wrong = jnp.max(jnp.where(good, 0.0, 1.0))

    @pl.when(wrong > 0.0)
    def again():
        queries, keys, values = mixed_t, grad_before.at[:, 0:D], g_t
        for src, dst in ((q_t, queries), (k_nat, keys), (v_t, values)):
            fetch = pltpu.make_async_copy(src, dst, out_sem)
            fetch.start()
            fetch.wait()
        if padded > length:
            hidden[length:, 0:WIDE_COLS] = jnp.zeros((padded - length, WIDE_COLS), bf16)
        qbd[...] = jnp.zeros(qbd.shape, bf16)
        for pair in range(HEADS // 2):

            @pl.loop(0, blocks)
            def block(step):
                attention_block(length, True, pair, block_of(step), queries, keys, values, out_t, totals, hidden, qbd)
                keep = pltpu.make_async_copy(
                    hidden.at[pl.ds(0, length), 0:WIDE_COLS], weights_out.at[step, pair], out_sem
                )
                keep.start()
                keep.wait()

    inverse_totals[...] = 1.0 / totals[...]
    place = lax.axis_index("narrow")
    counted[...] = jnp.zeros(counted.shape, f32)
    counted[:, CLASS_TOK:length] = counts[pl.ds(place, 1), :].astype(f32)
    head_parts = split(jnp.concatenate([head[...], jnp.zeros((5, D), f32)], axis=0))
    head_rows = jnp.concatenate(head_parts, axis=0)
    head_cols = jnp.concatenate([head_rows, jnp.zeros((128 - 16, D), bf16)], axis=0)
    head_deep = jnp.concatenate([head_parts[0], head_parts[1], head_parts[0], head_parts[1]], axis=0)

    @pl.loop(0, blocks // GROUP)
    def forward(step):
        spots = [block_of(step * GROUP + k) for k in range(GROUP)]
        middles, lows, befores, hids, results = [], [], [], [], []
        for here in spots:
            mixed = out_t[:, here].astype(bf16)
            mixed_t[:, here] = mixed
            middle = xbuf[here, :].astype(f32) + dot(mixed, w_out[...], TN)
            mid[here, :] = middle
            middles.append(middle)
        for here, middle in zip(spots, middles):
            xhat, _ = norm_parts(middle)
            low = (xhat * gain + shift).astype(bf16)
            act[here, :] = low
            lows.append(low)
        for here, low, middle in zip(spots, lows, middles):
            before = dot(low, w_up[...])
            square = before * before
            half = 0.5 + 0.5 * jnp.tanh(before * (GELU_A + (GELU_A * GELU_B) * square))
            wide = before * half
            hid = wide.astype(bf16)
            hidden[here, :] = hid
            bend = half + (wide - wide * half) * (2.0 * GELU_A + (6.0 * GELU_A * GELU_B) * square)
            slope[here, :] = bend
            results.append(middle + dot(hid, w_down[...]))
        for here, result in zip(spots, results):
            high, rest = split(result)
            res_high[here, :] = high
            res_rest[here, :] = rest
            found = dot(high, head_cols, NT) + dot(rest, head_cols, NT)
            found = found.T
            logits[:, here] = found[0:8, :] + found[8:16, :]

    send_out = pltpu.make_async_copy(res_high.at[pl.ds(0, length)], output, sem)
    send_out.start()
    genes = length - CLASS_TOK
    zero, disp, inflate = head_grads(
        (logits[0:1, :], logits[1:2, :], logits[2:3, :]),
        counted[...],
        jnp.full((1, 128), library[place].astype(f32))[:, 0:1],
        genes,
        length,
    )
    down_high, down_rest = split(jnp.concatenate([zero, disp, inflate, jnp.zeros((5, padded), f32)], axis=0))
    downs[0:8, :] = down_high
    downs[8:16, :] = down_rest

    @pl.loop(0, blocks // GROUP)
    def backward(step):
        spots = [block_of(step * GROUP + k) for k in range(GROUP)]
        grads, backs, twos, lows = [], [], [], []
        for here in spots:
            both = downs[:, here]
            deep = jnp.concatenate([both[0:8], both[0:8], both[8:16], both[8:16]], axis=0)
            grad_res = dot(deep, head_deep, TN)
            low = grad_res.astype(bf16)
            res_low[here, :] = low
            grads.append(grad_res)
            lows.append(low)
        for here, low in zip(spots, lows):
            back = (slope[here, :] * dot(low, w_down[...], NT)).astype(bf16)
            grad_before[here, :] = back
            backs.append(back)
        for back in backs:
            twos.append(dot(back, w_up[...], NT))
        lows = []
        for here, grad_two, grad_res in zip(spots, twos, grads):
            xhat, inverse = norm_parts(mid[here, :])
            grad_norm[0:8, :] += row_sums(grad_two * xhat)
            grad_norm[8:16, :] += row_sums(grad_two)
            total = grad_res + norm_back(xhat, inverse, gain, grad_two)
            mid[here, :] = total
            total_low = total.astype(bf16)
            mid_low[here, :] = total_low
            lows.append(total_low)
        for here, total_low in zip(spots, lows):
            grad_t = dot(w_out[...], total_low, NT).astype(bf16)
            g_t[:, here] = grad_t
            grad_t = grad_t.astype(f32)
            shares = [
                grad_t[h * HEAD_DIM : (h + 1) * HEAD_DIM] * inverse_totals[h : h + 1, here] for h in range(HEADS)
            ]
            g_nat[here, :] = jnp.concatenate(shares, axis=0).astype(bf16).T
            inner = grad_t * out_t[:, here]
            delta[:, here] = jnp.concatenate(
                [
                    jnp.sum(inner[h * HEAD_DIM : (h + 1) * HEAD_DIM], axis=0, keepdims=True)
                    for h in range(HEADS)
                ]
                + [jnp.zeros((8 - HEADS, BLK), f32)],
                axis=0,
            )

    sends = [
        pltpu.make_async_copy(src, dst, send_sems.at[index])
        for index, (src, dst) in enumerate(((mid, grad_mid), (g_nat, g_nat_out), (g_t, g_t_out)))
    ]
    for send in sends:
        send.start()
    found = dot(downs[...], res_high[...]) + dot(downs[...], res_rest[...])
    grad_head[...] = found[0:8, :] + found[8:16, :]
    used = 2 * D + HEAD_DIM
    if early.shape[2] > used:
        early_buf[:, :, used:, :] = jnp.zeros((2, 2, early.shape[2] - used, D), f32)

    def put(index, begin, end, pieces):
        for who in range(HEADS):
            early_buf[who % 2, who // 2, begin : begin + pieces[who].shape[0], :] = pieces[who]
        part = (slice(None), slice(None), pl.ds(begin, end - begin))
        return save((early_buf.at[part],), (early.at[part],), send_sems, index)

    grad = dot(res_low[...], hidden[...], TN)
    sends += put(3, 0, D, [grad[:, who * D : (who + 1) * D] for who in range(HEADS)])
    grad = dot(act[...], grad_before[...], TN)
    sends += put(4, D, 2 * D, [grad[:, who * D : (who + 1) * D] for who in range(HEADS)])
    grad = dot(mixed_t[...], mid_low[...])
    sends += put(
        5, 2 * D, early.shape[2], [grad[who * HEAD_DIM : (who + 1) * HEAD_DIM, :] for who in range(HEADS)]
    )
    for send in [send_out] + sends:
        send.wait()


def middle_stage(wide, tokens, out_t, totals, q_t, k_nat, v_t, weights, w_out, w_up, w_down, npar, head, counts, library):
    length = tokens.shape[1]
    padded = out_t.shape[1]
    shape = jax.ShapeDtypeStruct
    return pl.pallas_call(
        functools.partial(middle_kernel, length),
        out_shape=(
            shape((length, D), bf16),
            shape((padded, D), f32),
            shape((padded, D), bf16),
            shape((D, padded), bf16),
            shape((2, 2, early_rows(wide), D), f32),
            shape(weights.shape, bf16),
            shape((8, padded), f32),
            shape((8, padded), f32),
            shape((16, D), f32),
            shape((8, D), f32),
        ),
        in_specs=anywhere(2) + vmem(1) + anywhere(7) + vmem(3) + [pl.BlockSpec(memory_space=pltpu.SMEM)],
        out_specs=tuple(anywhere(6) + vmem(4)),
        input_output_aliases={6: 5},
        scratch_shapes=[
            pltpu.VMEM((padded, D), bf16),
            pltpu.VMEM((D, padded), f32),
            pltpu.VMEM((8, padded), f32),
            pltpu.VMEM((padded, D), bf16),
            pltpu.VMEM((D, padded), bf16),
            pltpu.VMEM((2, 2, early_rows(wide), D), f32),
            pltpu.VMEM((D, padded), bf16),
            pltpu.VMEM((padded, D), f32),
            pltpu.VMEM((padded, D), bf16),
            pltpu.VMEM((padded, D), bf16),
            pltpu.VMEM((padded, D), bf16),
            pltpu.VMEM((padded, FF), bf16),
            pltpu.VMEM((padded, FF), f32),
            pltpu.VMEM((padded, D), bf16),
            pltpu.VMEM((padded, FF), bf16),
            pltpu.VMEM((padded, D), bf16),
            pltpu.VMEM((8, padded), f32),
            pltpu.VMEM((16, padded), bf16),
            pltpu.VMEM((1, padded), f32),
            pltpu.VMEM((PAIR, WIDE_COLS), bf16),
            pltpu.VMEM(w_out.shape, bf16),
            pltpu.VMEM(w_up.shape, bf16),
            pltpu.VMEM(w_down.shape, bf16),
            pltpu.SemaphoreType.DMA,
            pltpu.SemaphoreType.DMA,
            pltpu.SemaphoreType.DMA((6,)),
        ],
        compiler_params=params(),
        name="middle",
    )(tokens, out_t, totals, q_t, k_nat, v_t, weights, w_out, w_up, w_down, npar, head, counts, library)


class Shares:
    def __init__(self, stack, bufs, sems, wide):
        self.stack = stack
        self.held, self.got, self.keep, self.send, self.come, self.parts, self.arrived, self.total = bufs
        self.sems, self.wide = sems, wide
        self.me, self.row, self.core, self.over, self.beside = narrow_mates()
        self.place = lax.axis_index("wide")

    def peer(self, step):
        return lax.rem(self.place + step, self.wide)

    def to_beside(self):
        return remote(self.stack.at[1 - self.core], self.got, self.sems, 0, "narrow", self.beside)

    def to_over(self):
        return remote(self.send, self.come, self.sems, 1, "narrow", self.over)

    def spread(self, step):
        peer = self.peer(step)
        return remote(
            self.parts.at[peer], self.arrived.at[self.place], self.sems, 1 + step, "wide", peer
        )

    def share(self, step):
        peer = self.peer(step)
        mine = self.total.at[self.place]
        return remote(mine, mine, self.sems, self.wide + step, "wide", peer)

    def start_beside(self):
        self.to_beside().start()

    def finish(self):
        for step in range(1, self.wide):
            self.share(step).wait_recv()

    def settle(self):
        self.to_beside().wait_send()
        self.to_over().wait_send()
        for step in range(1, self.wide):
            self.spread(step).wait_send()
            self.share(step).wait_send()

    def start_spreads(self):
        for step in range(1, self.wide):
            self.spread(step).start()
        self.arrived[self.place] = self.parts[self.place]

    def arrive(self):
        for step in range(1, self.wide):
            self.spread(step).wait_recv()
        return jnp.sum(self.arrived[...].astype(f32), axis=0)

    def start_shares(self, mine):
        self.total[self.place] = mine.astype(bf16)
        for step in range(1, self.wide):
            self.share(step).start()


class RowFirst(Shares):
    def start_over(self):
        self.to_beside().wait_recv()
        def both(row):
            return self.held[row].astype(f32) + self.got[row].astype(f32)

        self.send[...] = both(1 - self.row).astype(bf16)
        self.to_over().start()
        self.keep[...] = both(self.row)

    def start_spread(self):
        self.to_over().wait_recv()
        whole = (self.keep[...] + self.come[...].astype(f32)).astype(bf16)
        self.parts[...] = whole.reshape(self.parts.shape)
        self.start_spreads()

    def start_share(self):
        self.start_shares(self.arrive())


class WideFirst(Shares):
    def start_spread(self):
        self.to_beside().wait_recv()
        depth = self.parts.shape[2]
        for row in range(2):
            whole = (self.held[row] + self.got[row]).astype(bf16)
            for place in range(self.wide):
                self.parts[place, row] = whole[place * depth : (place + 1) * depth, :]
        self.start_spreads()

    def start_over(self):
        self.keep[...] = self.arrive()
        self.send[...] = self.keep[1 - self.row].astype(bf16)
        self.to_over().start()

    def start_share(self):
        self.to_over().wait_recv()
        self.start_shares(self.keep[self.row] + self.come[...].astype(f32))


def share_scratch(rows, wide, wide_first):
    depth = rows // wide
    if wide_first:
        shapes = [((2, rows, D), f32), ((2, rows, D), f32), ((2, depth, D), f32)]
        shapes += [((depth, D), bf16)] * 2 + [((wide, 2, depth, D), bf16)] * 2 + [((wide, depth, D), bf16)]
    else:
        shapes = [((2, rows, D), bf16), ((rows, D), f32)] + [((rows, D), bf16)] * 2 + [((wide, depth, D), bf16)] * 3
    return [pltpu.VMEM(*what) for what in shapes] + [pltpu.SemaphoreType.DMA((2, 2 * wide))]


SIDE = 1
STAGES = 3


def cuts_of(length):
    blocks = -(-length // BLK)
    stages = min(STAGES, blocks)
    return [blocks * k // stages for k in range(stages + 1)]


def phases_of(length):
    cuts = cuts_of(length)
    blocks, found = cuts[-1], []
    for k in range(len(cuts) - 1):
        begin, end = cuts[k] * BLK, min(cuts[k + 1] * BLK, length)
        if k + 2 == len(cuts):
            found.append((cuts[k], blocks, begin, length, "end", k))
        else:
            found.append((cuts[k], blocks, begin, end, "add" if k else "set", None))
            found.append((cuts[k], cuts[k + 1], end, length, "end", k))
    return found


def back_kernel(length, wide, *refs):
    tok, out_own, early, weights = refs[0:4]
    given = refs[4:12]
    inverse, delta, npar, norm_two, head_two = refs[12:17]
    out_all, grad_all, early_sum, late_sum, squares_out = refs[17:22]
    refs = refs[22:]
    xbuf, probs, dscore, gbd, qnd, gnd, dk, dv, dq_t, joined, grad_low, norm_one, late, squares = refs[0:14]
    sem, own_sems, out_sems, over_sems, beside_sems, pass_sems, square_sems = refs[14:21]
    early_bufs = refs[21:29]
    early_sems = refs[29]
    late_bufs = refs[30:37]
    late_sems = refs[37]
    taken = refs[38:46]
    taken_sems, weight_sems = refs[46:48]
    v_nat, k_t, q_nat, g_nat, g_t, x1, grad_mid, w_in = taken

    padded = x1.shape[0]
    blocks = padded // BLK
    phases = phases_of(length)
    me, row, core, over, beside = narrow_mates()
    soon = (cuts_of(length)[1] if blocks > 1 else blocks) * BLK

    def piece_of(index, ref, first_part):
        part = slice(0, soon) if first_part else slice(soon, None)
        return ref.at[part, :] if index in (0, 2, 3) else ref.at[:, part]

    def bring(first_part, first_sem):
        return save(
            [piece_of(index, given[index], first_part) for index in range(5)],
            [piece_of(index, taken[index], first_part) for index in range(5)],
            taken_sems,
            first_sem,
        )

    fetches = bring(True, 0)

    def width_of(index):
        count = phases[index][1] - phases[index][0]
        return SIDE if count % SIDE == 0 else 1

    def fetch(index, turn, slot):
        begins, _, begin, end = phases[index][0:4]
        return [
            pltpu.make_async_copy(
                weights.at[begins + turn * width_of(index) + k, pair, pl.ds(begin, end - begin)],
                probs.at[slot, k, pair, pl.ds(0, end - begin)],
                weight_sems.at[slot, k, pair],
            )
            for k in range(width_of(index))
            for pair in range(HEADS // 2)
        ]

    for one in fetch(0, 0, 0):
        one.start()
    fetches_next = bring(False, 8) if soon < padded else []
    fetches_late = save(given[5:8], taken[5:8], taken_sems, 5)
    copy = pltpu.make_async_copy(tok.at[me], xbuf.at[pl.ds(0, length)], sem)
    copy.start()
    hold = pltpu.make_async_copy(early.at[core], early_bufs[0], own_sems.at[0])
    hold.start()
    keep_out = pltpu.make_async_copy(out_own, out_all.at[me], own_sems.at[1])
    keep_out.start()
    greet(wide)
    first = WideFirst(early, early_bufs, early_sems, wide)
    last = RowFirst(late, (late.at[core],) + tuple(late_bufs), late_sems, wide)
    out_over = remote(out_own, out_all.at[me], out_sems, 0, "narrow", over)
    out_beside = remote(out_own, out_all.at[me], out_sems, 1, "narrow", beside)
    out_pass = remote(out_all.at[over], out_all.at[over], out_sems, 2, "narrow", beside)
    first.start_beside()
    out_over.start()
    out_beside.start()

    if padded > length:
        xbuf[length:, :] = jnp.zeros((padded - length, D), bf16)
        joined[length:, D:] = jnp.zeros((padded - length, 2 * D), bf16)
    dscore[...] = jnp.zeros(dscore.shape, bf16)
    for ref in (gbd, qnd, gnd):
        ref[...] = jnp.zeros(ref.shape, bf16)
    norm_one[...] = jnp.zeros(norm_one.shape, f32)
    dk[...] = jnp.zeros(dk.shape, f32)
    dv[...] = jnp.zeros(dv.shape, f32)
    scale = HEAD_DIM ** (-0.5)

    def begin():
        for one in fetches_next:
            one.wait()
        if padded > length:
            k_t[:, length:] = jnp.zeros((D, padded - length), bf16)
        hold.wait()
        first.start_spread()

    def hand_on():
        out_over.wait_recv()
        out_pass.start()

    def attention(steps, slot, start, stop, mode):
        spots = [block_of(step) for step in steps]
        size = stop - start
        whole = ceil_to(size, BLK)
        rows = key_chunk(size)

        def pairs_of(ref, pair, here):
            return jnp.concatenate([ref[2 * pair : 2 * pair + 1, here], ref[2 * pair + 1 : 2 * pair + 2, here]], axis=1)

        for pair in range(HEADS // 2):
            low = pair * PAIR
            mid = low + HEAD_DIM
            top = low + PAIR
            for k, here in enumerate(spots):
                gbd[k, pair, 0:HEAD_DIM, 0:BLK] = g_t[low:mid, here]
                gbd[k, pair, HEAD_DIM:PAIR, BLK:WIDE_COLS] = g_t[mid:top, here]
                both = q_nat[here, low:top]
                qnd[k, pair, 0:BLK, 0:HEAD_DIM] = both[:, 0:HEAD_DIM]
                qnd[k, pair, BLK:WIDE_COLS, HEAD_DIM:PAIR] = both[:, HEAD_DIM:PAIR]
                both = g_nat[here, low:top]
                gnd[k, pair, 0:BLK, 0:HEAD_DIM] = both[:, 0:HEAD_DIM]
                gnd[k, pair, BLK:WIDE_COLS, HEAD_DIM:PAIR] = both[:, HEAD_DIM:PAIR]
            for k, here in enumerate(spots):
                grads = gbd[k, pair]
                share = pairs_of(inverse, pair, here)
                inner = pairs_of(delta, pair, here)
                for at in range(0, size, rows):
                    part = slice(start + at, start + at + rows)
                    change = (dot(v_nat[part, low:top], grads) - inner) * share
                    weight = probs[slot, k, pair, at : at + rows, :].astype(f32)
                    dscore[k, at : at + rows, :] = (weight * change).astype(bf16)
            for k, here in enumerate(spots):
                dv[start:stop, low:top] += dot(probs[slot, k, pair, 0:size, :], gnd[k, pair])
            for k, here in enumerate(spots):
                dk[start:stop, low:top] += dot(dscore[k, 0:size, :], qnd[k, pair])
            for k, here in enumerate(spots):
                moved = dot(k_t[low:top, start : start + whole], dscore[k, 0:whole, :])
                one, two = moved[0:HEAD_DIM, 0:BLK], moved[HEAD_DIM:PAIR, BLK:WIDE_COLS]
                if mode != "set":
                    one = one + dq_t[low:mid, here]
                    two = two + dq_t[mid:top, here]
                if mode == "end":
                    joined[here, low:top] = (jnp.concatenate([one, two], axis=0) * scale).astype(bf16).T
                else:
                    dq_t[low:mid, here] = one
                    dq_t[mid:top, here] = two

    def run_phase(index, events):
        begins, ends, start, stop, mode, _ = phases[index]
        side = width_of(index)
        turns = (ends - begins) // side
        done = sum((p[1] - p[0]) // width_of(k) for k, p in enumerate(phases[:index]))

        @pl.loop(0, turns)
        def block(turn):
            slot = lax.rem(turn + done, 2)
            for when, event in events.items():
                pl.when(turn == when)(event)
            for one in fetch(index, turn, slot):
                one.wait()

            @pl.when(turn + 1 < turns)
            def ahead():
                for one in fetch(index, turn + 1, 1 - slot):
                    one.start()

            if index + 1 < len(phases):

                @pl.when(turn + 1 == turns)
                def across():
                    for one in fetch(index + 1, 0, 1 - slot):
                        one.start()

            attention([begins + turn * side + k for k in range(side)], slot, start, stop, mode)

    def settle_keys(start, stop):
        joined[start:stop, D : 2 * D] = (dk[start:stop, :] * scale).astype(bf16)
        joined[start:stop, 2 * D :] = dv[start:stop, :].astype(bf16)

    gain = npar[0:1, :]

    def close(steps):
        spots = [block_of(step) for step in steps]
        totals = [dot(joined[here, :], w_in[...].reshape(3 * D, D)) for here in spots]
        parts = [norm_parts(xbuf[here, :].astype(f32)) for here in spots]
        for here, total, (xhat, spread) in zip(spots, totals, parts):
            norm_one[0:8, :] += row_sums(total * xhat)
            norm_one[8:16, :] += row_sums(total)
            grad_low[here, :] = (grad_mid[here, :] + norm_back(xhat, spread, gain, total)).astype(bf16)

    def piece(index):
        return pl.ds(index * BLK, min(BLK, length - index * BLK))

    def chunk(index, who):
        return grad_all.at[who, piece(index)]

    def held(index):
        return grad_low.at[piece(index)]

    to_over = [remote(held(k), chunk(k, me), over_sems, k, "narrow", over) for k in range(blocks)]
    to_beside = [remote(held(k), chunk(k, me), beside_sems, k, "narrow", beside) for k in range(blocks)]
    passed = [remote(chunk(k, over), chunk(k, over), pass_sems, k, "narrow", beside) for k in range(blocks)]
    mine = pltpu.make_async_copy(grad_low.at[pl.ds(0, length)], grad_all.at[me], own_sems.at[2])

    for one in fetches:
        one.wait()
    events = [{} for _ in phases]
    events[0] = {min(3, blocks // width_of(0) - 1): begin}
    middle_phase = min(2 if len(phases) > 3 else 1, len(phases) - 1)
    events[middle_phase] = {0: first.start_over}
    cuts = cuts_of(length)
    sent = 0
    for index, (begins, ends, start, stop, mode, part) in enumerate(phases):
        run_phase(index, events[index])
        if index == middle_phase:
            hand_on()
        if part is None:
            continue
        settle_keys(cuts[part] * BLK, min(cuts[part + 1] * BLK, length))
        if part == 0:
            copy.wait()
            for one in fetches_late:
                one.wait()
        close(range(cuts[part], cuts[part + 1]))
        if part + 2 < len(cuts):
            sent = cuts[part + 1]
            for k in range(cuts[part], sent):
                to_over[k].start()
                to_beside[k].start()
        if part == max(0, len(cuts) - 3):
            first.start_share()

    late[...] = jnp.zeros(late.shape, bf16)
    grad_w = dot(x1[...], joined[...], TN)
    for which in range(3):
        turned = grad_w[:, which * D : (which + 1) * D].T.astype(bf16)
        for who in range(HEADS):
            late[who % 2, who // 2, which * HEAD_DIM : (which + 1) * HEAD_DIM, :] = turned[
                who * HEAD_DIM : (who + 1) * HEAD_DIM, :
            ]
    sums = [norm_one[0:8, :], norm_one[8:16, :], norm_two[0:8, :], norm_two[8:16, :]]
    extra = jnp.concatenate([jnp.sum(v, axis=0, keepdims=True) for v in sums] + [head_two[0:4, :]], axis=0)
    extra = jnp.concatenate([extra, jnp.zeros_like(extra)], axis=0).astype(bf16)
    for who in range(HEADS):
        late[who % 2, who // 2, 3 * HEAD_DIM : 3 * HEAD_DIM + 16, :] = extra
    last.start_beside()
    mine.start()
    first.finish()
    early_sum[...] = first.total[...].reshape(early_sum.shape)
    last.start_over()
    for k in range(sent, blocks):
        to_over[k].start()
        to_beside[k].start()
    last.start_spread()
    for k in range(sent):
        to_over[k].wait_recv()
        passed[k].start()
    last.start_share()
    last.finish()
    late_sum[...] = last.total[...].reshape(late_sum.shape)
    whole = early_sum[...].astype(f32)
    part = late_sum[0 : 3 * HEAD_DIM, :].astype(f32)
    level = jnp.sum(row_sums(whole * whole) + row_sums(part * part), axis=(0, 1), keepdims=True)
    squares[me] = jnp.broadcast_to(level, squares.shape[1:])
    told = []
    for index, mate in enumerate((over, beside, (1 - row) * 2 + 1 - core)):
        tell = remote(squares.at[me], squares.at[me], square_sems, index, "narrow", mate)
        tell.start()
        told.append(tell)
    for k in range(sent, blocks):
        to_over[k].wait_recv()
        passed[k].start()
    for tell in told:
        tell.wait_recv()
    squares_out[...] = squares[...]
    keep_out.wait()
    mine.wait()
    out_beside.wait_recv()
    out_pass.wait_recv()
    for k in range(blocks):
        to_beside[k].wait_recv()
        passed[k].wait_recv()
    for tell in told + [out_over, out_beside, out_pass] + to_over + to_beside + passed:
        tell.wait_send()
    first.settle()
    last.settle()


def back_stage(wide, tokens, out_own, early, weights, *rest):
    cells, length, _ = tokens.shape
    padded = rest[0].shape[0]
    blocks = padded // BLK
    reach = max(p[3] - p[2] for p in phases_of(length))
    shape = jax.ShapeDtypeStruct
    return pl.pallas_call(
        functools.partial(back_kernel, length, wide),
        out_shape=(
            shape((cells, length, D), bf16),
            shape((cells, length, D), bf16),
            shape((early_rows(wide), D), bf16),
            shape((late_rows(wide), D), bf16),
            shape((HEADS, 8, 128), f32),
        ),
        in_specs=anywhere(12) + vmem(5),
        out_specs=tuple(anywhere(2) + vmem(3)),
        scratch_shapes=[
            pltpu.VMEM((padded, D), bf16),
            pltpu.VMEM((2, SIDE, HEADS // 2, reach, WIDE_COLS), bf16),
            pltpu.VMEM((SIDE, ceil_to(reach, BLK), WIDE_COLS), bf16),
            pltpu.VMEM((SIDE, HEADS // 2, PAIR, WIDE_COLS), bf16),
            pltpu.VMEM((SIDE, HEADS // 2, WIDE_COLS, PAIR), bf16),
            pltpu.VMEM((SIDE, HEADS // 2, WIDE_COLS, PAIR), bf16),
            pltpu.VMEM((length, D), f32),
            pltpu.VMEM((length, D), f32),
            pltpu.VMEM((D, padded), f32),
            pltpu.VMEM((padded, 3 * D), bf16),
            pltpu.VMEM((padded, D), bf16),
            pltpu.VMEM((16, D), f32),
            pltpu.VMEM((2, 2, late_rows(wide), D), bf16),
            pltpu.VMEM((HEADS, 8, 128), f32),
            pltpu.SemaphoreType.DMA,
            pltpu.SemaphoreType.DMA((3,)),
            pltpu.SemaphoreType.DMA((2, 3)),
            pltpu.SemaphoreType.DMA((2, blocks)),
            pltpu.SemaphoreType.DMA((2, blocks)),
            pltpu.SemaphoreType.DMA((2, blocks)),
            pltpu.SemaphoreType.DMA((2, 3)),
        ]
        + share_scratch(early_rows(wide), wide, True)
        + share_scratch(late_rows(wide), wide, False)
        + [pltpu.VMEM(value.shape, value.dtype) for value in rest[0:8]]
        + [pltpu.SemaphoreType.DMA((13,)), pltpu.SemaphoreType.DMA((2, SIDE, HEADS // 2))],
        compiler_params=params(collective_id=2, has_side_effects=True),
        name="back",
    )(tokens, out_own, early, weights, *rest)


def adam_update(grad, first, second, weight, decay_rate, rate):
    first_new = decay_first * first + (1.0 - decay_first) * grad
    second_new = decay_second * second + (1.0 - decay_second) * grad * grad
    fix_first = 1.0 - decay_first**STEP
    fix_second = 1.0 - decay_second**STEP
    direction = first_new / fix_first / (jnp.sqrt(second_new / fix_second) + adam_eps)
    return (first_new, second_new, weight - rate * (direction + decay_rate * weight))


def finish_kernel(early, late, squares, *refs):
    sources, refs = refs[0:26], refs[26:]
    outputs, input_grad, grad_norm_ref = refs[0:3]
    targets, refs = refs[3:33], refs[33:]
    ins, refs = refs[0:24], refs[24:]
    outs, refs = refs[0:30], refs[30:]
    low, wide_out, same, in_sems, out_sems, low_sems, wide_sems, same_sems = refs
    out_all, grad_all = sources[24:26]
    cells, length, _ = grad_all.shape
    slots, deep, _ = low.shape
    pieces = [(cell, at) for cell in range(cells) for at in range(0, length, deep)]

    def load(index):
        cell, at = pieces[index]
        return pltpu.make_async_copy(grad_all.at[cell, pl.ds(at, deep)], low.at[index % slots], low_sems.at[index % slots])

    def store(index):
        cell, at = pieces[index]
        return pltpu.make_async_copy(
            wide_out.at[index % slots], input_grad.at[cell, pl.ds(at, deep)], wide_sems.at[index % slots]
        )

    def carry(index, out):
        cell, at = pieces[index]
        slot = same.at[index % slots]
        if out:
            return pltpu.make_async_copy(slot, outputs.at[cell, pl.ds(at, deep)], same_sems.at[1, index % slots])
        return pltpu.make_async_copy(out_all.at[cell, pl.ds(at, deep)], slot, same_sems.at[0, index % slots])

    def move(index):
        load(index).wait()
        if index >= slots:
            store(index - slots).wait()
        wide_out[index % slots] = low[index % slots].astype(f32)
        store(index).start()
        if index + slots < len(pieces):
            load(index + slots).start()
        carry(index, False).wait()
        carry(index, True).start()
        back = index - 2
        if back >= 0 and back + slots < len(pieces):
            carry(back, True).wait()
            carry(back + slots, False).start()

    early_pieces = min(slots, len(pieces))
    for index in range(early_pieces):
        load(index).start()
        carry(index, False).start()
    fetches = save(sources[0:24], ins, in_sems, 0)
    for index in range(early_pieces):
        move(index)
    for fetch in fetches:
        fetch.wait()
    place = lax.axis_index("wide")
    whole = early[...].astype(f32)
    small = late[...].astype(f32)
    extra = small[3 * HEAD_DIM : 3 * HEAD_DIM + 8, :]
    live = lax.broadcasted_iota(jnp.int32, extra.shape, 0) < 7
    extra = jnp.where(live, extra, 0.0)
    shards = jnp.sum(squares[...], axis=0)[0:1, 0:1]
    grad_norm = jnp.sqrt(shards + jnp.sum(extra * extra, axis=(0, 1), keepdims=True))
    grad_norm_ref[...] = grad_norm
    factor = jnp.minimum(1.0, clip_limit / grad_norm)
    grads = (
        None,
        whole[2 * D : 2 * D + HEAD_DIM, :],
        whole[D : 2 * D, :],
        whole[0:D, :].T,
        extra[0:4, :],
        extra[4:7, :],
    )
    decays = (weight_decay,) * 4 + (0.0, weight_decay)
    rates = (learn_rate,) * 4 + (norm_rate, learn_rate)

    def update(index, grad, at):
        weight, first, second = ins[index][at], ins[6 + index][at], ins[12 + index][at]
        clipped = grad * factor
        first_new, second_new, weight_new = adam_update(clipped, first, second, weight, decays[index], rates[index])
        outs[5 * index][at] = clipped
        outs[5 * index + 1][at] = first_new
        outs[5 * index + 2][at] = second_new
        outs[5 * index + 3][at] = weight_new
        return weight_new

    def mean(index, at, piece):
        outs[5 * index + 4][at] = ema_keep * ins[18 + index][at] + (1.0 - ema_keep) * piece

    def rows_here(values, count):
        return pltpu.roll(values, lax.rem(D - place * count, D), 0)[0:count, :]

    for which in range(3):
        weight_new = update(0, small[which * HEAD_DIM : (which + 1) * HEAD_DIM, :], which)
        mean(0, which, rows_here(weight_new.T, ins[18].shape[1]))
    for index in range(1, 4):
        weight_new = update(index, grads[index], Ellipsis)
        mean(index, Ellipsis, rows_here(weight_new if index == 2 else weight_new.T, ins[18 + index].shape[0]))
    for index in range(4, 6):
        weight_new = update(index, grads[index], Ellipsis)
        rows, count = ins[18 + index].shape
        full = jnp.concatenate([weight_new, jnp.zeros((8 - rows, D), f32)], axis=0)
        turned = pltpu.roll(full, lax.rem(D - place * count, D), 1)
        mean(index, Ellipsis, turned[0:rows, 0:count])

    stores = save(outs, targets, out_sems, 0)
    for index in range(early_pieces, len(pieces)):
        move(index)
    for index in range(max(0, len(pieces) - slots), len(pieces)):
        store(index).wait()
    for index in range(max(0, len(pieces) - slots), len(pieces)):
        carry(index, True).wait()
    for copy in stores:
        copy.wait()


def finish(early, late, squares, state, out_all, grad_all):
    shape = jax.ShapeDtypeStruct
    outs = []
    for index in range(6):
        outs += [(state[index].shape, f32)] * 4 + [(state[18 + index].shape, f32)]
    rows = 736 if grad_all.shape[1] % 736 == 0 else key_chunk(grad_all.shape[1])
    slots = 6
    return pl.pallas_call(
        finish_kernel,
        out_shape=tuple(
            [shape(out_all.shape, bf16), shape(grad_all.shape, f32), shape((1, 1), f32)] + [shape(*what) for what in outs]
        ),
        in_specs=vmem(3) + anywhere(26),
        out_specs=tuple(anywhere(2) + vmem(1) + anywhere(30)),
        scratch_shapes=[pltpu.VMEM(value.shape, f32) for value in state]
        + [pltpu.VMEM(*what) for what in outs]
        + [
            pltpu.VMEM((slots, rows, D), bf16),
            pltpu.VMEM((slots, rows, D), f32),
            pltpu.VMEM((slots, rows, D), bf16),
            pltpu.SemaphoreType.DMA((24,)),
            pltpu.SemaphoreType.DMA((30,)),
            pltpu.SemaphoreType.DMA((slots,)),
            pltpu.SemaphoreType.DMA((slots,)),
            pltpu.SemaphoreType.DMA((2, slots)),
        ],
        compiler_params=params(),
        name="finish",
    )(early, late, squares, *state, out_all, grad_all)


def on_device(cell_tokens, library_size, gene_counts, *state):
    turn = lambda v: jnp.swapaxes(v, -1, -2)
    state = tuple(turn(v) if index in (0, 6, 12, 19, 21) else v for index, v in enumerate(state))
    attend_in, attend_out, up_weight, down_weight, norm_params, head_weight = state[0:6]
    wide = lax.axis_size("wide")
    w_out, w_up, w_down, weights, x1, k_nat, v_nat, q_nat, q_t, k_t, v_t, w_in, out_t, totals = front(
        cell_tokens, attend_in, attend_out, up_weight, down_weight, norm_params
    )
    out_own, grad_mid, g_nat, g_t, early, weights, delta, inverse, norm_two, head_two = middle_stage(
        wide,
        cell_tokens,
        out_t,
        totals,
        q_t,
        k_nat,
        v_t,
        weights,
        w_out,
        w_up,
        w_down,
        norm_params,
        head_weight,
        gene_counts,
        library_size,
    )
    out_all, grad_all, early, late, squares = back_stage(
        wide,
        cell_tokens,
        out_own,
        early,
        weights,
        v_nat,
        k_t,
        q_nat,
        g_nat,
        g_t,
        x1,
        grad_mid,
        w_in,
        inverse,
        delta,
        norm_params,
        norm_two,
        head_two,
    )
    output, input_grad, grad_norm, *updates = finish(early, late, squares, state, out_all, grad_all)
    updates = [turn(v) if index in (0, 1, 2, 3, 9, 19) else v for index, v in enumerate(updates)]
    return (output, input_grad, grad_norm.reshape(()), *updates)


def solution(mesh):
    by_in, by_rows, by_cols = P(None, None, "narrow"), P("narrow", None), P(None, "narrow")
    kinds = (by_in, by_rows, by_cols, by_rows, P(), P())
    means = (
        P(None, "wide", "narrow"),
        P("narrow", "wide"),
        P("wide", "narrow"),
        P("narrow", "wide"),
        P(None, "wide"),
        P(None, "wide"),
    )
    cell = P("wide", None, None)
    outs = (cell, cell, P())
    for kind, mean in zip(kinds, means):
        outs += (kind, kind, kind, kind, mean)
    return jax.shard_map(
        on_device,
        mesh=mesh,
        in_specs=(cell, P("wide"), P("wide", None)) + kinds * 3 + means,
        out_specs=outs,
        check_vma=False,
    )
```

```python
import functools

import jax
import jax.numpy as jnp
from jax import lax
from jax.experimental import pallas as pl
from jax.experimental.pallas import tpu as pltpu
from jax.sharding import PartitionSpec as P

D = 256
FF = 1024
HEADS = 4
HEAD_DIM = 64
CLASS_TOK = 8
STEP = 10

layer_eps = 1e-05
clip_limit = 0.25
decay_first = 0.9
decay_second = 0.999
learn_rate = 0.06
norm_rate = 0.6
adam_eps = 1e-08
weight_decay = 0.01
ema_keep = 0.75

f32 = jnp.float32
bf16 = jnp.bfloat16

NN = (((1,), (0,)), ((), ()))
NT = (((1,), (1,)), ((), ()))
TN = (((0,), (0,)), ((), ()))

BLK = 256
PAIR = 2 * HEAD_DIM
WIDE_COLS = 2 * BLK
LOG2E = 1.4426950408889634
SCORE = LOG2E * HEAD_DIM ** (-0.5)
GELU_A = 0.7978845608028654
GELU_B = 0.044715
GROUP = 3
VMEM_BYTES = 60 * 2**20


def dot(left, right, dims=NN, precision=None):
    return lax.dot_general(left, right, dims, precision=precision, preferred_element_type=f32)


def ceil_to(value, unit):
    return -(-value // unit) * unit


def key_chunk(length):
    for rows in (368, 464, 320, 592, 256, 224, 288, 208, 176, 128, 64, 48, 32, 16):
        if length % rows == 0:
            return rows
    return length


def vmem(count):
    return [pl.BlockSpec(memory_space=pltpu.VMEM)] * count


def params(**more):
    return pltpu.CompilerParams(vmem_limit_bytes=VMEM_BYTES, **more)


def anywhere(count):
    return [pl.BlockSpec(memory_space=pl.ANY)] * count


def remote(src, dst, sems, index, axis, peer):
    return pltpu.make_async_remote_copy(
        src_ref=src,
        dst_ref=dst,
        send_sem=sems.at[0, index],
        recv_sem=sems.at[1, index],
        device_id={axis: peer},
        device_id_type=pl.DeviceIdType.MESH,
    )


def narrow_mates():
    me = lax.axis_index("narrow")
    row, core = me // 2, me % 2
    return me, row, core, (1 - row) * 2 + core, row * 2 + 1 - core


def greet(wide_peers=0):
    _, _, _, over, beside = narrow_mates()
    barrier = pltpu.get_barrier_semaphore()
    mesh_id = pl.DeviceIdType.MESH
    pl.semaphore_signal(barrier, inc=1, device_id={"narrow": over}, device_id_type=mesh_id)
    pl.semaphore_signal(barrier, inc=1, device_id={"narrow": beside}, device_id_type=mesh_id)
    if wide_peers:
        place = lax.axis_index("wide")
        _, row, core, _, _ = narrow_mates()
        pl.semaphore_signal(
            barrier, inc=1, device_id={"narrow": (1 - row) * 2 + 1 - core}, device_id_type=mesh_id
        )
        for step in range(1, wide_peers):
            peer = lax.rem(place + step, wide_peers)
            pl.semaphore_signal(barrier, inc=1, device_id={"wide": peer}, device_id_type=mesh_id)
    pl.semaphore_wait(barrier, 2 + (wide_peers if wide_peers else 0))


def norm_parts(values):
    center = values - jnp.mean(values, axis=-1, keepdims=True)
    spread = jnp.mean(center * center, axis=-1, keepdims=True)
    inverse = lax.rsqrt(spread + layer_eps)
    return center * inverse, inverse


def norm_back(xhat, inverse, gain, grad):
    scaled = gain * grad
    mean_one = jnp.mean(scaled, axis=-1, keepdims=True)
    mean_two = jnp.mean(scaled * xhat, axis=-1, keepdims=True)
    return inverse * (scaled - mean_one - xhat * mean_two)


def row_sums(values):
    return jnp.sum(values.reshape(-1, 8, values.shape[-1]), axis=0)


def block_of(step, width=BLK):
    if isinstance(step, int):
        return pl.ds(step * width, width)
    return pl.ds(pl.multiple_of(step * width, width), width)


def attention_block(length, shifted, pair, here, q_t, k_nat, v_t, out_t, totals, probs, qbd):
    rows = key_chunk(length)
    low = pair * PAIR
    qbd[0:HEAD_DIM, 0:BLK] = q_t[low : low + HEAD_DIM, here]
    qbd[HEAD_DIM:PAIR, BLK:WIDE_COLS] = q_t[low + HEAD_DIM : low + PAIR, here]
    queries = qbd[...]

    def scores(start):
        return dot(k_nat[start : start + rows, low : low + PAIR], queries) * SCORE

    top = jnp.zeros((1, WIDE_COLS), f32)
    if shifted:
        top = jnp.full((1, WIDE_COLS), -jnp.inf, f32)
        for start in range(0, length, rows):
            top = jnp.maximum(top, jnp.max(scores(start), axis=0, keepdims=True))
    total = jnp.zeros((8, WIDE_COLS), f32)
    for start in range(0, length, rows):
        score = scores(start)
        weight = jnp.exp2(score - top) if shifted else jnp.exp2(score)
        total = total + row_sums(weight)
        probs[start : start + rows, 0:WIDE_COLS] = weight.astype(bf16)
    total = jnp.sum(total, axis=0, keepdims=True)
    mixed = dot(v_t[low : low + PAIR, :], probs[:, 0:WIDE_COLS]) / total
    out_t[low : low + HEAD_DIM, here] = mixed[0:HEAD_DIM, 0:BLK]
    out_t[low + HEAD_DIM : low + PAIR, here] = mixed[HEAD_DIM:PAIR, BLK:WIDE_COLS]
    totals[2 * pair : 2 * pair + 1, here] = total[:, 0:BLK]
    totals[2 * pair + 1 : 2 * pair + 2, here] = total[:, BLK:WIDE_COLS]


def front_kernel(
    length,
    tok,
    far_in,
    far_out,
    far_up,
    far_down,
    npar,
    w_out,
    w_up,
    w_down,
    *refs,
):
    weights, outs, refs = refs[0], refs[1:11], refs[11:]
    x1, k_nat, v_nat, q_nat, q_t, k_t, v_t, w_in, out_t, totals = refs[0:10]
    xbuf, probs, qbd, low_out, low_up, low_down, sem, own_sem, over_sem, beside_sem, pass_sem, save_sems = refs[10:22]
    weight_sems = refs[22]
    own_in, own_out, own_up, own_down = refs[23:27]
    padded = x1.shape[0]
    blocks = padded // BLK
    me, _, _, over, beside = narrow_mates()
    gets = save((far_in,), (own_in,), own_sem, 0)
    copy = pltpu.make_async_copy(tok.at[me], xbuf.at[pl.ds(0, length)], sem)
    copy.start()
    gets += save((far_out, far_up, far_down), (own_out, own_up, own_down), own_sem, 1)

    def slot(index, who):
        if index == 0:
            return w_in.at[:, pl.ds(pl.multiple_of(who * HEAD_DIM, HEAD_DIM), HEAD_DIM), :]
        if index == 1:
            return w_out.at[pl.ds(pl.multiple_of(who * HEAD_DIM, HEAD_DIM), HEAD_DIM), :]
        if index == 2:
            return w_up.at[:, pl.ds(pl.multiple_of(who * D, D), D)]
        return w_down.at[pl.ds(pl.multiple_of(who * D, D), D), :]

    def source(index):
        return (slot(0, me), low_out, low_up, low_down)[index]

    gets[0].wait()
    for which in range(3):
        w_in[which, pl.ds(pl.multiple_of(me * HEAD_DIM, HEAD_DIM), HEAD_DIM), :] = own_in[which].astype(bf16)
    greet()
    to_over = [remote(source(k), slot(k, me), over_sem, k, "narrow", over) for k in range(4)]
    to_beside = [remote(source(k), slot(k, me), beside_sem, k, "narrow", beside) for k in range(4)]
    passed = [remote(slot(k, over), slot(k, over), pass_sem, k, "narrow", beside) for k in range(4)]
    mine = [pltpu.make_async_copy(source(k), slot(k, me), own_sem.at[k]) for k in range(1, 4)]
    to_over[0].start()
    to_beside[0].start()
    for get in gets[1:]:
        get.wait()
    low_out[...] = own_out[...].astype(bf16)
    low_up[...] = own_up[...].astype(bf16)
    low_down[...] = own_down[...].astype(bf16)

    if padded > length:
        xbuf[length:, :] = jnp.zeros((padded - length, D), bf16)
        probs[:, :, length:, :] = jnp.zeros((2, HEADS // 2, padded - length, WIDE_COLS), bf16)
    qbd[...] = jnp.zeros(qbd.shape, bf16)
    totals[...] = jnp.ones(totals.shape, f32)
    copy.wait()
    gain = npar[0:1, :]
    shift = npar[1:2, :]

    @pl.loop(0, blocks)
    def norm(step):
        here = block_of(step)
        xhat, _ = norm_parts(xbuf[here, :].astype(f32))
        x1[here, :] = (xhat * gain + shift).astype(bf16)

    to_over[0].wait_recv()
    passed[0].start()
    for k in range(1, 4):
        to_over[k].start()
        to_beside[k].start()
        mine[k - 1].start()
    to_beside[0].wait_recv()
    passed[0].wait_recv()

    @pl.loop(0, blocks // GROUP)
    def project(step):
        here = block_of(step, GROUP * BLK)
        act = x1[here, :]
        q_nat[here, :] = dot(act, w_in[0], NT).astype(bf16)
        k_nat[here, :] = dot(act, w_in[1], NT).astype(bf16)
        v_nat[here, :] = dot(act, w_in[2], NT).astype(bf16)
        q_t[:, here] = dot(w_in[0], act, NT).astype(bf16)
        k_t[:, here] = dot(w_in[1], act, NT).astype(bf16)
        v_t[:, here] = dot(w_in[2], act, NT).astype(bf16)

    if padded > length:
        v_t[:, length:] = jnp.zeros((D, padded - length), bf16)

    half = (blocks // 2) * BLK

    def keep(step, pair, slot):
        return pltpu.make_async_copy(
            probs.at[slot, pair, pl.ds(0, length)], weights.at[step, pair], weight_sems.at[slot, pair]
        )

    def attend(step):
        here = block_of(step)
        slot = lax.rem(step, 2)

        @pl.when(step >= 2)
        def free():
            for pair in range(HEADS // 2):
                keep(step - 2, pair, slot).wait()

        for pair in range(HEADS // 2):
            attention_block(
                length, False, pair, here, q_t, k_nat, v_t, out_t, totals, probs.at[slot, pair], qbd.at[pair]
            )
            keep(step, pair, slot).start()

    saves = save((x1, k_nat, v_nat, q_nat, q_t, k_t, v_t, w_in), outs[0:8], save_sems, 0)
    pl.loop(0, blocks // 2)(attend)
    for k in range(1, 4):
        to_over[k].wait_recv()
        passed[k].start()
    saves += save((out_t.at[:, 0:half],), (outs[8].at[:, 0:half],), save_sems, 8)
    pl.loop(blocks // 2, blocks)(attend)
    saves += save((out_t.at[:, half:], totals), (outs[8].at[:, half:], outs[9]), save_sems, 9)
    for step in range(max(0, blocks - 2), blocks):
        for pair in range(HEADS // 2):
            keep(step, pair, step % 2).wait()
    for copy in saves:
        copy.wait()
    for k in range(1, 4):
        to_beside[k].wait_recv()
        passed[k].wait_recv()
        mine[k - 1].wait()
    for k in range(4):
        to_over[k].wait_send()
        to_beside[k].wait_send()
        passed[k].wait_send()


def save(sources, targets, sems, first):
    copies = [
        pltpu.make_async_copy(src, dst, sems.at[first + k]) for k, (src, dst) in enumerate(zip(sources, targets))
    ]
    for copy in copies:
        copy.start()
    return copies


def front(tokens, own_in, own_out, own_up, own_down, npar):
    length = tokens.shape[1]
    padded = ceil_to(length, BLK)
    shape = jax.ShapeDtypeStruct
    kept = (
        [((padded, D), bf16)] * 4
        + [((D, padded), bf16)] * 3
        + [((3, D, D), bf16), ((D, padded), f32), ((8, padded), f32)]
    )
    return pl.pallas_call(
        functools.partial(front_kernel, length),
        out_shape=tuple(
            [shape((D, D), bf16), shape((D, FF), bf16), shape((FF, D), bf16)]
            + [shape((padded // BLK, HEADS // 2, length, WIDE_COLS), bf16)]
            + [shape(*what) for what in kept]
        ),
        in_specs=anywhere(5) + vmem(1),
        out_specs=tuple(anywhere(14)),
        scratch_shapes=[pltpu.VMEM(*what) for what in kept]
        + [
            pltpu.VMEM((padded, D), bf16),
            pltpu.VMEM((2, HEADS // 2, padded, WIDE_COLS), bf16),
            pltpu.VMEM((HEADS // 2, PAIR, WIDE_COLS), bf16),
            pltpu.VMEM(own_out.shape, bf16),
            pltpu.VMEM(own_up.shape, bf16),
            pltpu.VMEM(own_down.shape, bf16),
            pltpu.SemaphoreType.DMA,
            pltpu.SemaphoreType.DMA((4,)),
            pltpu.SemaphoreType.DMA((2, 4)),
            pltpu.SemaphoreType.DMA((2, 4)),
            pltpu.SemaphoreType.DMA((2, 4)),
            pltpu.SemaphoreType.DMA((11,)),
            pltpu.SemaphoreType.DMA((2, HEADS // 2)),
            pltpu.VMEM(own_in.shape, f32),
            pltpu.VMEM(own_out.shape, f32),
            pltpu.VMEM(own_up.shape, f32),
            pltpu.VMEM(own_down.shape, f32),
        ],
        compiler_params=params(collective_id=1, has_side_effects=True),
        name="front",
    )(tokens, own_in, own_out, own_up, own_down, npar)


def shared_rows(rows, wide):
    return ceil_to(-(-rows // wide), 16) * wide


def early_rows(wide):
    return shared_rows(2 * D + HEAD_DIM, wide)


def late_rows(wide):
    return shared_rows(3 * HEAD_DIM + 16, wide)


def split(values):
    high = values.astype(bf16)
    return high, (values - high.astype(f32)).astype(bf16)


def softplus(values):
    return jnp.maximum(values, 0.0) + jnp.log1p(jnp.exp(-jnp.abs(values)))


def sigmoid(values):
    return 1.0 / (1.0 + jnp.exp(-values))


def head_grads(logits, counts, library, genes, length):
    lane = lax.broadcasted_iota(jnp.int32, logits[0].shape, 1)
    valid = (lane >= CLASS_TOK) & (lane < length)
    mean_logit = jnp.where(valid, logits[0], -jnp.inf)
    top = jnp.max(mean_logit, axis=1, keepdims=True)
    raised = jnp.exp(mean_logit - top)
    total = jnp.sum(raised, axis=1, keepdims=True)
    share = raised / total
    log_mean = jnp.where(valid, logits[0], 0.0) - top - jnp.log(total) + jnp.log(library)
    disp = 0.5 + softplus(logits[1])
    log_disp = jnp.log(disp)
    inflate = logits[2]
    gap = log_mean - log_disp
    mean_part = sigmoid(gap)
    disp_part = sigmoid(-gap)
    log_both = jnp.maximum(log_disp, log_mean) + jnp.log1p(jnp.exp(-jnp.abs(gap)))
    shared = disp * (log_disp - log_both)
    shared_disp = (log_disp - log_both) + mean_part
    shared_mean = -disp * mean_part
    none = counts == 0.0
    lean = sigmoid(shared - inflate)
    psi = jnp.zeros_like(disp)
    for step in range(7):
        psi = psi + jnp.where(counts > step, 1.0 / (disp + step), 0.0)
    grad_disp = jnp.where(none, -lean * shared_disp, counts * disp_part / disp - shared_disp - psi)
    grad_mean = jnp.where(none, -lean * shared_mean, -shared_mean - counts * disp_part)
    grad_inflate = jnp.where(none, lean - sigmoid(-inflate), sigmoid(inflate))
    part = 1.0 / genes
    grad_disp = jnp.where(valid, grad_disp * part, 0.0)
    grad_mean = jnp.where(valid, grad_mean * part, 0.0)
    grad_inflate = jnp.where(valid, grad_inflate * part, 0.0)
    grad_zero = grad_mean - share * jnp.sum(grad_mean, axis=1, keepdims=True)
    return (grad_zero, grad_disp * sigmoid(logits[1]), grad_inflate)


def middle_kernel(
    length,
    tok,
    first_out_t,
    first_totals,
    q_t,
    k_nat,
    v_t,
    weights,
    far_out,
    far_up,
    far_down,
    npar,
    head,
    counts,
    library,
    output,
    grad_mid,
    g_nat_out,
    g_t_out,
    early,
    weights_out,
    outputs,
    delta,
    inverse_totals,
    grad_norm,
    grad_head,
    xbuf,
    out_t,
    totals,
    g_nat,
    g_t,
    early_buf,
    mixed_t,
    mid,
    res_high,
    res_rest,
    act,
    hidden,
    slope,
    res_low,
    grad_before,
    mid_low,
    logits,
    downs,
    counted,
    qbd,
    w_out,
    w_up,
    w_down,
    sem,
    out_sem,
    send_sems,
):
    padded = xbuf.shape[0]
    blocks = padded // BLK
    me = lax.axis_index("narrow")
    copy = pltpu.make_async_copy(tok.at[me], xbuf.at[pl.ds(0, length)], sem)
    copy.start()
    get_out = pltpu.make_async_copy(first_out_t, out_t, out_sem)
    get_out.start()
    get_weights = save((far_out, far_up, far_down), (w_out, w_up, w_down), send_sems, 0)
    if padded > length:
        xbuf[length:, :] = jnp.zeros((padded - length, D), bf16)
    grad_norm[...] = jnp.zeros(grad_norm.shape, f32)
    copy.wait()
    get_out.wait()
    for get in get_weights:
        get.wait()
    gain = npar[2:3, :]
    shift = npar[3:4, :]

    level = first_totals[...]
    totals[...] = level
    good = (level > 1e-25) & (level < 1e36)
    wrong = jnp.max(jnp.where(good, 0.0, 1.0))

    @pl.when(wrong > 0.0)
    def again():
        queries, keys, values = mixed_t, grad_before.at[:, 0:D], g_t
        for src, dst in ((q_t, queries), (k_nat, keys), (v_t, values)):
            fetch = pltpu.make_async_copy(src, dst, out_sem)
            fetch.start()
            fetch.wait()
        if padded > length:
            hidden[length:, 0:WIDE_COLS] = jnp.zeros((padded - length, WIDE_COLS), bf16)
        qbd[...] = jnp.zeros(qbd.shape, bf16)
        for pair in range(HEADS // 2):

            @pl.loop(0, blocks)
            def block(step):
                attention_block(length, True, pair, block_of(step), queries, keys, values, out_t, totals, hidden, qbd)
                keep = pltpu.make_async_copy(
                    hidden.at[pl.ds(0, length), 0:WIDE_COLS], weights_out.at[step, pair], out_sem
                )
                keep.start()
                keep.wait()

    inverse_totals[...] = 1.0 / totals[...]
    place = lax.axis_index("narrow")
    counted[...] = jnp.zeros(counted.shape, f32)
    counted[:, CLASS_TOK:length] = counts[pl.ds(place, 1), :].astype(f32)
    head_parts = split(jnp.concatenate([head[...], jnp.zeros((5, D), f32)], axis=0))
    head_rows = jnp.concatenate(head_parts, axis=0)
    head_cols = jnp.concatenate([head_rows, jnp.zeros((128 - 16, D), bf16)], axis=0)
    head_deep = jnp.concatenate([head_parts[0], head_parts[1], head_parts[0], head_parts[1]], axis=0)

    @pl.loop(0, blocks // GROUP)
    def forward(step):
        spots = [block_of(step * GROUP + k) for k in range(GROUP)]
        middles, lows, befores, hids, results = [], [], [], [], []
        for here in spots:
            mixed = out_t[:, here].astype(bf16)
            mixed_t[:, here] = mixed
            middle = xbuf[here, :].astype(f32) + dot(mixed, w_out[...], TN)
            mid[here, :] = middle
            middles.append(middle)
        for here, middle in zip(spots, middles):
            xhat, _ = norm_parts(middle)
            low = (xhat * gain + shift).astype(bf16)
            act[here, :] = low
            lows.append(low)
        for here, low, middle in zip(spots, lows, middles):
            before = dot(low, w_up[...])
            square = before * before
            half = 0.5 + 0.5 * jnp.tanh(before * (GELU_A + (GELU_A * GELU_B) * square))
            wide = before * half
            hid = wide.astype(bf16)
            hidden[here, :] = hid
            bend = half + (wide - wide * half) * (2.0 * GELU_A + (6.0 * GELU_A * GELU_B) * square)
            slope[here, :] = bend
            results.append(middle + dot(hid, w_down[...]))
        for here, result in zip(spots, results):
            high, rest = split(result)
            res_high[here, :] = high
            res_rest[here, :] = rest
            found = dot(high, head_cols, NT) + dot(rest, head_cols, NT)
            found = found.T
            logits[:, here] = found[0:8, :] + found[8:16, :]

    send_out = save(
        [res_high.at[pl.ds(0, length)]] * 2, [output, outputs.at[lax.axis_index("narrow")]], send_sems, 6
    )
    genes = length - CLASS_TOK
    zero, disp, inflate = head_grads(
        (logits[0:1, :], logits[1:2, :], logits[2:3, :]),
        counted[...],
        jnp.full((1, 128), library[place].astype(f32))[:, 0:1],
        genes,
        length,
    )
    down_high, down_rest = split(jnp.concatenate([zero, disp, inflate, jnp.zeros((5, padded), f32)], axis=0))
    downs[0:8, :] = down_high
    downs[8:16, :] = down_rest

    @pl.loop(0, blocks // GROUP)
    def backward(step):
        spots = [block_of(step * GROUP + k) for k in range(GROUP)]
        grads, backs, twos, lows = [], [], [], []
        for here in spots:
            both = downs[:, here]
            deep = jnp.concatenate([both[0:8], both[0:8], both[8:16], both[8:16]], axis=0)
            grad_res = dot(deep, head_deep, TN)
            low = grad_res.astype(bf16)
            res_low[here, :] = low
            grads.append(grad_res)
            lows.append(low)
        for here, low in zip(spots, lows):
            back = (slope[here, :] * dot(low, w_down[...], NT)).astype(bf16)
            grad_before[here, :] = back
            backs.append(back)
        for back in backs:
            twos.append(dot(back, w_up[...], NT))
        lows = []
        for here, grad_two, grad_res in zip(spots, twos, grads):
            xhat, inverse = norm_parts(mid[here, :])
            grad_norm[0:8, :] += row_sums(grad_two * xhat)
            grad_norm[8:16, :] += row_sums(grad_two)
            total = grad_res + norm_back(xhat, inverse, gain, grad_two)
            mid[here, :] = total
            total_low = total.astype(bf16)
            mid_low[here, :] = total_low
            lows.append(total_low)
        for here, total_low in zip(spots, lows):
            grad_t = dot(w_out[...], total_low, NT).astype(bf16)
            g_t[:, here] = grad_t
            grad_t = grad_t.astype(f32)
            shares = [
                grad_t[h * HEAD_DIM : (h + 1) * HEAD_DIM] * inverse_totals[h : h + 1, here] for h in range(HEADS)
            ]
            g_nat[here, :] = jnp.concatenate(shares, axis=0).astype(bf16).T
            inner = grad_t * out_t[:, here]
            delta[:, here] = jnp.concatenate(
                [
                    jnp.sum(inner[h * HEAD_DIM : (h + 1) * HEAD_DIM], axis=0, keepdims=True)
                    for h in range(HEADS)
                ]
                + [jnp.zeros((8 - HEADS, BLK), f32)],
                axis=0,
            )

    sends = [
        pltpu.make_async_copy(src, dst, send_sems.at[index])
        for index, (src, dst) in enumerate(((mid, grad_mid), (g_nat, g_nat_out), (g_t, g_t_out)))
    ]
    for send in sends:
        send.start()
    found = dot(downs[...], res_high[...]) + dot(downs[...], res_rest[...])
    grad_head[...] = found[0:8, :] + found[8:16, :]
    used = 2 * D + HEAD_DIM
    if early.shape[2] > used:
        early_buf[:, :, used:, :] = jnp.zeros((2, 2, early.shape[2] - used, D), f32)

    def put(index, begin, end, pieces):
        for who in range(HEADS):
            early_buf[who % 2, who // 2, begin : begin + pieces[who].shape[0], :] = pieces[who]
        part = (slice(None), slice(None), pl.ds(begin, end - begin))
        return save((early_buf.at[part],), (early.at[part],), send_sems, index)

    grad = dot(res_low[...], hidden[...], TN)
    sends += put(3, 0, D, [grad[:, who * D : (who + 1) * D] for who in range(HEADS)])
    grad = dot(act[...], grad_before[...], TN)
    sends += put(4, D, 2 * D, [grad[:, who * D : (who + 1) * D] for who in range(HEADS)])
    grad = dot(mixed_t[...], mid_low[...])
    sends += put(
        5, 2 * D, early.shape[2], [grad[who * HEAD_DIM : (who + 1) * HEAD_DIM, :] for who in range(HEADS)]
    )
    for send in send_out + sends:
        send.wait()


def middle_stage(wide, tokens, out_t, totals, q_t, k_nat, v_t, weights, w_out, w_up, w_down, npar, head, counts, library):
    length = tokens.shape[1]
    padded = out_t.shape[1]
    shape = jax.ShapeDtypeStruct
    return pl.pallas_call(
        functools.partial(middle_kernel, length),
        out_shape=(
            shape((length, D), bf16),
            shape((padded, D), f32),
            shape((padded, D), bf16),
            shape((D, padded), bf16),
            shape((2, 2, early_rows(wide), D), f32),
            shape(weights.shape, bf16),
            shape(tokens.shape, bf16),
            shape((8, padded), f32),
            shape((8, padded), f32),
            shape((16, D), f32),
            shape((8, D), f32),
        ),
        in_specs=anywhere(2) + vmem(1) + anywhere(7) + vmem(3) + [pl.BlockSpec(memory_space=pltpu.SMEM)],
        out_specs=tuple(anywhere(7) + vmem(4)),
        input_output_aliases={6: 5},
        scratch_shapes=[
            pltpu.VMEM((padded, D), bf16),
            pltpu.VMEM((D, padded), f32),
            pltpu.VMEM((8, padded), f32),
            pltpu.VMEM((padded, D), bf16),
            pltpu.VMEM((D, padded), bf16),
            pltpu.VMEM((2, 2, early_rows(wide), D), f32),
            pltpu.VMEM((D, padded), bf16),
            pltpu.VMEM((padded, D), f32),
            pltpu.VMEM((padded, D), bf16),
            pltpu.VMEM((padded, D), bf16),
            pltpu.VMEM((padded, D), bf16),
            pltpu.VMEM((padded, FF), bf16),
            pltpu.VMEM((padded, FF), f32),
            pltpu.VMEM((padded, D), bf16),
            pltpu.VMEM((padded, FF), bf16),
            pltpu.VMEM((padded, D), bf16),
            pltpu.VMEM((8, padded), f32),
            pltpu.VMEM((16, padded), bf16),
            pltpu.VMEM((1, padded), f32),
            pltpu.VMEM((PAIR, WIDE_COLS), bf16),
            pltpu.VMEM(w_out.shape, bf16),
            pltpu.VMEM(w_up.shape, bf16),
            pltpu.VMEM(w_down.shape, bf16),
            pltpu.SemaphoreType.DMA,
            pltpu.SemaphoreType.DMA,
            pltpu.SemaphoreType.DMA((8,)),
        ],
        compiler_params=params(),
        name="middle",
    )(tokens, out_t, totals, q_t, k_nat, v_t, weights, w_out, w_up, w_down, npar, head, counts, library)


class Shares:
    def __init__(self, stack, bufs, sems, wide):
        self.stack = stack
        self.held, self.got, self.keep, self.send, self.come, self.parts, self.arrived, self.total = bufs
        self.sems, self.wide = sems, wide
        self.me, self.row, self.core, self.over, self.beside = narrow_mates()
        self.place = lax.axis_index("wide")

    def peer(self, step):
        return lax.rem(self.place + step, self.wide)

    def to_beside(self):
        return remote(self.stack.at[1 - self.core], self.got, self.sems, 0, "narrow", self.beside)

    def to_over(self):
        return remote(self.send, self.come, self.sems, 1, "narrow", self.over)

    def spread(self, step):
        peer = self.peer(step)
        return remote(
            self.parts.at[peer], self.arrived.at[self.place], self.sems, 1 + step, "wide", peer
        )

    def share(self, step):
        peer = self.peer(step)
        mine = self.total.at[self.place]
        return remote(mine, mine, self.sems, self.wide + step, "wide", peer)

    def start_beside(self):
        self.to_beside().start()

    def finish(self):
        for step in range(1, self.wide):
            self.share(step).wait_recv()

    def settle(self):
        self.to_beside().wait_send()
        self.to_over().wait_send()
        for step in range(1, self.wide):
            self.spread(step).wait_send()
            self.share(step).wait_send()

    def start_spreads(self):
        for step in range(1, self.wide):
            self.spread(step).start()
        self.arrived[self.place] = self.parts[self.place]

    def arrive(self):
        for step in range(1, self.wide):
            self.spread(step).wait_recv()
        return jnp.sum(self.arrived[...].astype(f32), axis=0)

    def start_shares(self, mine):
        self.total[self.place] = mine.astype(bf16)
        for step in range(1, self.wide):
            self.share(step).start()


class RowFirst(Shares):
    def start_over(self):
        self.to_beside().wait_recv()
        def both(row):
            return self.held[row].astype(f32) + self.got[row].astype(f32)

        self.send[...] = both(1 - self.row).astype(bf16)
        self.to_over().start()
        self.keep[...] = both(self.row)

    def start_spread(self, extra):
        self.to_over().wait_recv()
        whole = self.keep[...] + self.come[...].astype(f32)
        begin, end = 3 * HEAD_DIM, 3 * HEAD_DIM + 16
        whole = jnp.concatenate([whole[0:begin], extra, jnp.zeros((8, D), f32), whole[end:]], axis=0).astype(bf16)
        self.parts[...] = whole.reshape(self.parts.shape)
        self.start_spreads()

    def start_share(self):
        self.start_shares(self.arrive())


class WideFirst(Shares):
    def start_spread(self):
        self.to_beside().wait_recv()
        depth = self.parts.shape[2]
        for row in range(2):
            whole = (self.held[row] + self.got[row]).astype(bf16)
            for place in range(self.wide):
                self.parts[place, row] = whole[place * depth : (place + 1) * depth, :]
        self.start_spreads()

    def start_over(self):
        self.keep[...] = self.arrive()
        self.send[...] = self.keep[1 - self.row].astype(bf16)
        self.to_over().start()

    def start_share(self):
        self.to_over().wait_recv()
        self.start_shares(self.keep[self.row] + self.come[...].astype(f32))


def share_scratch(rows, wide, wide_first):
    depth = rows // wide
    if wide_first:
        shapes = [((2, rows, D), f32), ((2, rows, D), f32), ((2, depth, D), f32)]
        shapes += [((depth, D), bf16)] * 2 + [((wide, 2, depth, D), bf16)] * 2 + [((wide, depth, D), bf16)]
    else:
        shapes = [((2, rows, D), bf16), ((rows, D), f32)] + [((rows, D), bf16)] * 2 + [((wide, depth, D), bf16)] * 3
    return [pltpu.VMEM(*what) for what in shapes] + [pltpu.SemaphoreType.DMA((2, 2 * wide))]


SIDE = 1
STAGES = 3


def cuts_of(length):
    blocks = -(-length // BLK)
    stages = min(STAGES, blocks)
    return [blocks * k // stages for k in range(stages + 1)]


def phases_of(length):
    cuts = cuts_of(length)
    blocks, found = cuts[-1], []
    for k in range(len(cuts) - 1):
        begin, end = cuts[k] * BLK, min(cuts[k + 1] * BLK, length)
        if k + 2 == len(cuts):
            found.append((cuts[k], blocks, begin, length, "end", k))
        else:
            found.append((cuts[k], blocks, begin, end, "add" if k else "set", None))
            found.append((cuts[k], cuts[k + 1], end, length, "end", k))
    return found


def back_kernel(length, wide, *refs):
    tok, out_own, early, weights = refs[0:4]
    given = refs[4:12]
    inverse, delta, npar, norm_two, head_two = refs[12:17]
    out_all, grad_all, early_sum, late_sum, squares_out = refs[17:22]
    refs = refs[22:]
    xbuf, probs, dscore, gbd, qnd, gnd, dk, dv, dq_t, joined, grad_low, norm_one, late, squares = refs[0:14]
    sem, own_sems, out_sems, over_sems, beside_sems, pass_sems, square_sems = refs[14:21]
    early_bufs = refs[21:29]
    early_sems = refs[29]
    late_bufs = refs[30:37]
    late_sems = refs[37]
    taken = refs[38:46]
    taken_sems, weight_sems, fellows, fellow_sems = refs[46:50]
    v_nat, k_t, q_nat, g_nat, g_t, x1, grad_mid, w_in = taken

    padded = x1.shape[0]
    blocks = padded // BLK
    phases = phases_of(length)
    me, row, core, over, beside = narrow_mates()
    soon = (cuts_of(length)[1] if blocks > 1 else blocks) * BLK

    def piece_of(index, ref, first_part):
        part = slice(0, soon) if first_part else slice(soon, None)
        return ref.at[part, :] if index in (0, 2, 3) else ref.at[:, part]

    def bring(first_part, first_sem):
        return save(
            [piece_of(index, given[index], first_part) for index in range(5)],
            [piece_of(index, taken[index], first_part) for index in range(5)],
            taken_sems,
            first_sem,
        )

    fetches = bring(True, 0)

    def width_of(index):
        count = phases[index][1] - phases[index][0]
        return SIDE if count % SIDE == 0 else 1

    def fetch(index, turn, slot):
        begins, _, begin, end = phases[index][0:4]
        return [
            pltpu.make_async_copy(
                weights.at[begins + turn * width_of(index) + k, pair, pl.ds(begin, end - begin)],
                probs.at[slot, k, pair, pl.ds(0, end - begin)],
                weight_sems.at[slot, k, pair],
            )
            for k in range(width_of(index))
            for pair in range(HEADS // 2)
        ]

    for one in fetch(0, 0, 0):
        one.start()
    fetches_next = bring(False, 8) if soon < padded else []
    fetches_late = save(given[5:8], taken[5:8], taken_sems, 5)
    copy = pltpu.make_async_copy(tok.at[me], xbuf.at[pl.ds(0, length)], sem)
    copy.start()
    hold = pltpu.make_async_copy(early.at[core], early_bufs[0], own_sems.at[0])
    hold.start()
    greet(wide)
    first = WideFirst(early, early_bufs, early_sems, wide)
    last = RowFirst(late, (late.at[core],) + tuple(late_bufs), late_sems, wide)
    out_over = remote(out_own, out_all.at[me], out_sems, 0, "narrow", over)
    out_beside = remote(out_own, out_all.at[me], out_sems, 1, "narrow", beside)
    out_pass = remote(out_all.at[over], out_all.at[over], out_sems, 2, "narrow", beside)
    first.start_beside()
    out_over.start()
    out_beside.start()

    if padded > length:
        xbuf[length:, :] = jnp.zeros((padded - length, D), bf16)
        joined[length:, D:] = jnp.zeros((padded - length, 2 * D), bf16)
    dscore[...] = jnp.zeros(dscore.shape, bf16)
    for ref in (gbd, qnd, gnd):
        ref[...] = jnp.zeros(ref.shape, bf16)
    norm_one[...] = jnp.zeros(norm_one.shape, f32)
    dk[...] = jnp.zeros(dk.shape, f32)
    dv[...] = jnp.zeros(dv.shape, f32)
    scale = HEAD_DIM ** (-0.5)

    def begin():
        for one in fetches_next:
            one.wait()
        if padded > length:
            k_t[:, length:] = jnp.zeros((D, padded - length), bf16)
        hold.wait()
        first.start_spread()

    def hand_on():
        out_over.wait_recv()
        out_pass.start()

    def attention(steps, slot, start, stop, mode):
        spots = [block_of(step) for step in steps]
        size = stop - start
        whole = ceil_to(size, BLK)
        rows = key_chunk(size)

        def pairs_of(ref, pair, here):
            return jnp.concatenate([ref[2 * pair : 2 * pair + 1, here], ref[2 * pair + 1 : 2 * pair + 2, here]], axis=1)

        for pair in range(HEADS // 2):
            low = pair * PAIR
            mid = low + HEAD_DIM
            top = low + PAIR
            for k, here in enumerate(spots):
                gbd[k, pair, 0:HEAD_DIM, 0:BLK] = g_t[low:mid, here]
                gbd[k, pair, HEAD_DIM:PAIR, BLK:WIDE_COLS] = g_t[mid:top, here]
                both = q_nat[here, low:top]
                qnd[k, pair, 0:BLK, 0:HEAD_DIM] = both[:, 0:HEAD_DIM]
                qnd[k, pair, BLK:WIDE_COLS, HEAD_DIM:PAIR] = both[:, HEAD_DIM:PAIR]
                both = g_nat[here, low:top]
                gnd[k, pair, 0:BLK, 0:HEAD_DIM] = both[:, 0:HEAD_DIM]
                gnd[k, pair, BLK:WIDE_COLS, HEAD_DIM:PAIR] = both[:, HEAD_DIM:PAIR]
            for k, here in enumerate(spots):
                grads = gbd[k, pair]
                share = pairs_of(inverse, pair, here)
                inner = pairs_of(delta, pair, here)
                for at in range(0, size, rows):
                    part = slice(start + at, start + at + rows)
                    change = (dot(v_nat[part, low:top], grads) - inner) * share
                    weight = probs[slot, k, pair, at : at + rows, :].astype(f32)
                    dscore[k, at : at + rows, :] = (weight * change).astype(bf16)
            for k, here in enumerate(spots):
                dv[start:stop, low:top] += dot(probs[slot, k, pair, 0:size, :], gnd[k, pair])
            for k, here in enumerate(spots):
                dk[start:stop, low:top] += dot(dscore[k, 0:size, :], qnd[k, pair])
            for k, here in enumerate(spots):
                moved = dot(k_t[low:top, start : start + whole], dscore[k, 0:whole, :])
                one, two = moved[0:HEAD_DIM, 0:BLK], moved[HEAD_DIM:PAIR, BLK:WIDE_COLS]
                if mode != "set":
                    one = one + dq_t[low:mid, here]
                    two = two + dq_t[mid:top, here]
                if mode == "end":
                    joined[here, low:top] = (jnp.concatenate([one, two], axis=0) * scale).astype(bf16).T
                else:
                    dq_t[low:mid, here] = one
                    dq_t[mid:top, here] = two

    def run_phase(index, events):
        begins, ends, start, stop, mode, _ = phases[index]
        side = width_of(index)
        turns = (ends - begins) // side
        done = sum((p[1] - p[0]) // width_of(k) for k, p in enumerate(phases[:index]))

        @pl.loop(0, turns)
        def block(turn):
            slot = lax.rem(turn + done, 2)
            for when, event in events.items():
                pl.when(turn == when)(event)
            for one in fetch(index, turn, slot):
                one.wait()

            @pl.when(turn + 1 < turns)
            def ahead():
                for one in fetch(index, turn + 1, 1 - slot):
                    one.start()

            if index + 1 < len(phases):

                @pl.when(turn + 1 == turns)
                def across():
                    for one in fetch(index + 1, 0, 1 - slot):
                        one.start()

            attention([begins + turn * side + k for k in range(side)], slot, start, stop, mode)

    def settle_keys(start, stop):
        joined[start:stop, D : 2 * D] = (dk[start:stop, :] * scale).astype(bf16)
        joined[start:stop, 2 * D :] = dv[start:stop, :].astype(bf16)

    gain = npar[0:1, :]

    def close(steps):
        spots = [block_of(step) for step in steps]
        totals = [dot(joined[here, :], w_in[...].reshape(3 * D, D)) for here in spots]
        parts = [norm_parts(xbuf[here, :].astype(f32)) for here in spots]
        for here, total, (xhat, spread) in zip(spots, totals, parts):
            norm_one[0:8, :] += row_sums(total * xhat)
            norm_one[8:16, :] += row_sums(total)
            grad_low[here, :] = (grad_mid[here, :] + norm_back(xhat, spread, gain, total)).astype(bf16)

    def piece(index):
        return pl.ds(index * BLK, min(BLK, length - index * BLK))

    def chunk(index, who):
        return grad_all.at[who, piece(index)]

    def held(index):
        return grad_low.at[piece(index)]

    to_over = [remote(held(k), chunk(k, me), over_sems, k, "narrow", over) for k in range(blocks)]
    to_beside = [remote(held(k), chunk(k, me), beside_sems, k, "narrow", beside) for k in range(blocks)]
    passed = [remote(chunk(k, over), chunk(k, over), pass_sems, k, "narrow", beside) for k in range(blocks)]
    mine = pltpu.make_async_copy(grad_low.at[pl.ds(0, length)], grad_all.at[me], own_sems.at[2])

    for one in fetches:
        one.wait()
    events = [{} for _ in phases]
    events[0] = {min(3, blocks // width_of(0) - 1): begin}
    middle_phase = min(2 if len(phases) > 3 else 1, len(phases) - 1)
    events[middle_phase] = {0: first.start_over}
    cuts = cuts_of(length)
    sent = 0
    for index, (begins, ends, start, stop, mode, part) in enumerate(phases):
        run_phase(index, events[index])
        if index == middle_phase:
            hand_on()
        if part is None:
            continue
        settle_keys(cuts[part] * BLK, min(cuts[part + 1] * BLK, length))
        if part == 0:
            copy.wait()
            for one in fetches_late:
                one.wait()
        if part + 2 < len(cuts):
            close(range(cuts[part], cuts[part + 1]))
            sent = cuts[part + 1]
            for k in range(cuts[part], sent):
                to_over[k].start()
                to_beside[k].start()
        if part == max(0, len(cuts) - 3):
            first.start_share()

    late[...] = jnp.zeros(late.shape, bf16)
    grad_w = dot(x1[...], joined[...], TN)
    for which in range(3):
        turned = grad_w[:, which * D : (which + 1) * D].T.astype(bf16)
        for who in range(HEADS):
            late[who % 2, who // 2, which * HEAD_DIM : (which + 1) * HEAD_DIM, :] = turned[
                who * HEAD_DIM : (who + 1) * HEAD_DIM, :
            ]
    last.start_beside()
    close(range(cuts[-2], cuts[-1]))
    sums = [norm_one[0:8, :], norm_one[8:16, :], norm_two[0:8, :], norm_two[8:16, :]]
    fellows[me] = jnp.concatenate([jnp.sum(v, axis=0, keepdims=True) for v in sums] + [head_two[0:4, :]], axis=0)
    last.start_over()
    gossip = []
    for index, mate in enumerate((over, beside, (1 - row) * 2 + 1 - core)):
        gossip.append(remote(fellows.at[me], fellows.at[me], fellow_sems, index, "narrow", mate))
        gossip[-1].start()
    mine.start()
    first.finish()
    early_sum[...] = first.total[...].reshape(early_sum.shape)
    for k in range(sent, blocks):
        to_over[k].start()
        to_beside[k].start()
    for tell in gossip:
        tell.wait_recv()
    last.start_spread(jnp.sum(fellows[...], axis=0))
    for k in range(sent):
        to_over[k].wait_recv()
        passed[k].start()
    last.start_share()
    last.finish()
    late_sum[...] = last.total[...].reshape(late_sum.shape)
    whole = early_sum[...].astype(f32)
    part = late_sum[0 : 3 * HEAD_DIM, :].astype(f32)
    level = jnp.sum(row_sums(whole * whole) + row_sums(part * part), axis=(0, 1), keepdims=True)
    squares[me] = jnp.broadcast_to(level, squares.shape[1:])
    told = []
    for index, mate in enumerate((over, beside, (1 - row) * 2 + 1 - core)):
        tell = remote(squares.at[me], squares.at[me], square_sems, index, "narrow", mate)
        tell.start()
        told.append(tell)
    for k in range(sent, blocks):
        to_over[k].wait_recv()
        passed[k].start()
    for tell in told:
        tell.wait_recv()
    squares_out[...] = squares[...]
    mine.wait()
    out_beside.wait_recv()
    out_pass.wait_recv()
    for k in range(blocks):
        to_beside[k].wait_recv()
        passed[k].wait_recv()
    for tell in gossip + told + [out_over, out_beside, out_pass] + to_over + to_beside + passed:
        tell.wait_send()
    first.settle()
    last.settle()


def back_stage(wide, tokens, out_own, early, weights, *rest):
    cells, length, _ = tokens.shape
    padded = rest[0].shape[0]
    blocks = padded // BLK
    reach = max(p[3] - p[2] for p in phases_of(length))
    shape = jax.ShapeDtypeStruct
    return pl.pallas_call(
        functools.partial(back_kernel, length, wide),
        out_shape=(
            shape((cells, length, D), bf16),
            shape((cells, length, D), bf16),
            shape((early_rows(wide), D), bf16),
            shape((late_rows(wide), D), bf16),
            shape((HEADS, 8, 128), f32),
        ),
        in_specs=anywhere(12) + vmem(5),
        out_specs=tuple(anywhere(2) + vmem(3)),
        scratch_shapes=[
            pltpu.VMEM((padded, D), bf16),
            pltpu.VMEM((2, SIDE, HEADS // 2, reach, WIDE_COLS), bf16),
            pltpu.VMEM((SIDE, ceil_to(reach, BLK), WIDE_COLS), bf16),
            pltpu.VMEM((SIDE, HEADS // 2, PAIR, WIDE_COLS), bf16),
            pltpu.VMEM((SIDE, HEADS // 2, WIDE_COLS, PAIR), bf16),
            pltpu.VMEM((SIDE, HEADS // 2, WIDE_COLS, PAIR), bf16),
            pltpu.VMEM((length, D), f32),
            pltpu.VMEM((length, D), f32),
            pltpu.VMEM((D, padded), f32),
            pltpu.VMEM((padded, 3 * D), bf16),
            pltpu.VMEM((padded, D), bf16),
            pltpu.VMEM((16, D), f32),
            pltpu.VMEM((2, 2, late_rows(wide), D), bf16),
            pltpu.VMEM((HEADS, 8, 128), f32),
            pltpu.SemaphoreType.DMA,
            pltpu.SemaphoreType.DMA((3,)),
            pltpu.SemaphoreType.DMA((2, 3)),
            pltpu.SemaphoreType.DMA((2, blocks)),
            pltpu.SemaphoreType.DMA((2, blocks)),
            pltpu.SemaphoreType.DMA((2, blocks)),
            pltpu.SemaphoreType.DMA((2, 3)),
        ]
        + share_scratch(early_rows(wide), wide, True)
        + share_scratch(late_rows(wide), wide, False)
        + [pltpu.VMEM(value.shape, value.dtype) for value in rest[0:8]]
        + [pltpu.SemaphoreType.DMA((13,)), pltpu.SemaphoreType.DMA((2, SIDE, HEADS // 2))]
        + [pltpu.VMEM((HEADS, 8, D), f32), pltpu.SemaphoreType.DMA((2, HEADS - 1))],
        compiler_params=params(collective_id=2, has_side_effects=True),
        name="back",
    )(tokens, out_own, early, weights, *rest)


def adam_update(grad, first, second, weight, decay_rate, rate):
    first_new = decay_first * first + (1.0 - decay_first) * grad
    second_new = decay_second * second + (1.0 - decay_second) * grad * grad
    fix_first = 1.0 - decay_first**STEP
    fix_second = 1.0 - decay_second**STEP
    direction = first_new / fix_first / (jnp.sqrt(second_new / fix_second) + adam_eps)
    return (first_new, second_new, weight - rate * (direction + decay_rate * weight))


def finish_kernel(early, late, squares, *refs):
    sources, refs = refs[0:26], refs[27:]
    outputs, input_grad, grad_norm_ref = refs[0:3]
    targets, refs = refs[3:33], refs[33:]
    ins, refs = refs[0:24], refs[24:]
    outs, refs = refs[0:30], refs[30:]
    low, wide_out, same, in_sems, out_sems, low_sems, wide_sems, same_sems = refs
    out_all, grad_all = sources[24:26]
    cells, length, _ = grad_all.shape
    slots, deep, _ = low.shape
    pieces = [(cell, at) for cell in range(cells) for at in range(0, length, deep)]

    def load(index):
        cell, at = pieces[index]
        return pltpu.make_async_copy(grad_all.at[cell, pl.ds(at, deep)], low.at[index % slots], low_sems.at[index % slots])

    def store(index):
        cell, at = pieces[index]
        return pltpu.make_async_copy(
            wide_out.at[index % slots], input_grad.at[cell, pl.ds(at, deep)], wide_sems.at[index % slots]
        )

    me = lax.axis_index("narrow")
    carried = len(pieces) * (cells - 1) // cells

    def carry(index, out):
        cell, at = pieces[index]
        cell = lax.rem(me + 1 + cell, cells)
        slot = same.at[index % slots]
        if out:
            return pltpu.make_async_copy(slot, outputs.at[cell, pl.ds(at, deep)], same_sems.at[1, index % slots])
        return pltpu.make_async_copy(out_all.at[cell, pl.ds(at, deep)], slot, same_sems.at[0, index % slots])

    def move(index):
        load(index).wait()
        if index >= slots:
            store(index - slots).wait()
        wide_out[index % slots] = low[index % slots].astype(f32)
        store(index).start()
        if index + slots < len(pieces):
            load(index + slots).start()
        if index >= carried:
            return
        carry(index, False).wait()
        carry(index, True).start()
        back = index - 2
        if back >= 0 and back + slots < carried:
            carry(back, True).wait()
            carry(back + slots, False).start()

    early_pieces = min(slots, len(pieces))
    for index in range(early_pieces):
        load(index).start()
        if index < carried:
            carry(index, False).start()
    fetches = save(sources[0:24], ins, in_sems, 0)
    for index in range(early_pieces):
        move(index)
    for fetch in fetches:
        fetch.wait()
    place = lax.axis_index("wide")
    whole = early[...].astype(f32)
    small = late[...].astype(f32)
    extra = small[3 * HEAD_DIM : 3 * HEAD_DIM + 8, :]
    live = lax.broadcasted_iota(jnp.int32, extra.shape, 0) < 7
    extra = jnp.where(live, extra, 0.0)
    shards = jnp.sum(squares[...], axis=0)[0:1, 0:1]
    grad_norm = jnp.sqrt(shards + jnp.sum(extra * extra, axis=(0, 1), keepdims=True))
    grad_norm_ref[...] = grad_norm
    factor = jnp.minimum(1.0, clip_limit / grad_norm)
    grads = (
        None,
        whole[2 * D : 2 * D + HEAD_DIM, :],
        whole[D : 2 * D, :],
        whole[0:D, :].T,
        extra[0:4, :],
        extra[4:7, :],
    )
    decays = (weight_decay,) * 4 + (0.0, weight_decay)
    rates = (learn_rate,) * 4 + (norm_rate, learn_rate)

    def update(index, grad, at):
        weight, first, second = ins[index][at], ins[6 + index][at], ins[12 + index][at]
        clipped = grad * factor
        first_new, second_new, weight_new = adam_update(clipped, first, second, weight, decays[index], rates[index])
        outs[5 * index][at] = clipped
        outs[5 * index + 1][at] = first_new
        outs[5 * index + 2][at] = second_new
        outs[5 * index + 3][at] = weight_new
        return weight_new

    def mean(index, at, piece):
        outs[5 * index + 4][at] = ema_keep * ins[18 + index][at] + (1.0 - ema_keep) * piece

    def rows_here(values, count):
        return pltpu.roll(values, lax.rem(D - place * count, D), 0)[0:count, :]

    for which in range(3):
        weight_new = update(0, small[which * HEAD_DIM : (which + 1) * HEAD_DIM, :], which)
        mean(0, which, rows_here(weight_new.T, ins[18].shape[1]))
    for index in range(1, 4):
        weight_new = update(index, grads[index], Ellipsis)
        mean(index, Ellipsis, rows_here(weight_new if index == 2 else weight_new.T, ins[18 + index].shape[0]))
    for index in range(4, 6):
        weight_new = update(index, grads[index], Ellipsis)
        rows, count = ins[18 + index].shape
        full = jnp.concatenate([weight_new, jnp.zeros((8 - rows, D), f32)], axis=0)
        turned = pltpu.roll(full, lax.rem(D - place * count, D), 1)
        mean(index, Ellipsis, turned[0:rows, 0:count])

    stores = save(outs, targets, out_sems, 0)
    for index in range(early_pieces, len(pieces)):
        move(index)
    for index in range(max(0, len(pieces) - slots), len(pieces)):
        store(index).wait()
    for index in range(max(0, carried - slots), carried):
        carry(index, True).wait()
    for copy in stores:
        copy.wait()


def finish(early, late, squares, state, out_all, grad_all, outputs):
    shape = jax.ShapeDtypeStruct
    outs = []
    for index in range(6):
        outs += [(state[index].shape, f32)] * 4 + [(state[18 + index].shape, f32)]
    rows = 736 if grad_all.shape[1] % 736 == 0 else key_chunk(grad_all.shape[1])
    slots = 6
    return pl.pallas_call(
        finish_kernel,
        out_shape=tuple(
            [shape(out_all.shape, bf16), shape(grad_all.shape, f32), shape((1, 1), f32)] + [shape(*what) for what in outs]
        ),
        in_specs=vmem(3) + anywhere(27),
        input_output_aliases={29: 0},
        out_specs=tuple(anywhere(2) + vmem(1) + anywhere(30)),
        scratch_shapes=[pltpu.VMEM(value.shape, f32) for value in state]
        + [pltpu.VMEM(*what) for what in outs]
        + [
            pltpu.VMEM((slots, rows, D), bf16),
            pltpu.VMEM((slots, rows, D), f32),
            pltpu.VMEM((slots, rows, D), bf16),
            pltpu.SemaphoreType.DMA((24,)),
            pltpu.SemaphoreType.DMA((30,)),
            pltpu.SemaphoreType.DMA((slots,)),
            pltpu.SemaphoreType.DMA((slots,)),
            pltpu.SemaphoreType.DMA((2, slots)),
        ],
        compiler_params=params(),
        name="finish",
    )(early, late, squares, *state, out_all, grad_all, outputs)


def on_device(cell_tokens, library_size, gene_counts, *state):
    turn = lambda v: jnp.swapaxes(v, -1, -2)
    state = tuple(turn(v) if index in (0, 6, 12, 19, 21) else v for index, v in enumerate(state))
    attend_in, attend_out, up_weight, down_weight, norm_params, head_weight = state[0:6]
    wide = lax.axis_size("wide")
    w_out, w_up, w_down, weights, x1, k_nat, v_nat, q_nat, q_t, k_t, v_t, w_in, out_t, totals = front(
        cell_tokens, attend_in, attend_out, up_weight, down_weight, norm_params
    )
    out_own, grad_mid, g_nat, g_t, early, weights, outputs, delta, inverse, norm_two, head_two = middle_stage(
        wide,
        cell_tokens,
        out_t,
        totals,
        q_t,
        k_nat,
        v_t,
        weights,
        w_out,
        w_up,
        w_down,
        norm_params,
        head_weight,
        gene_counts,
        library_size,
    )
    out_all, grad_all, early, late, squares = back_stage(
        wide,
        cell_tokens,
        out_own,
        early,
        weights,
        v_nat,
        k_t,
        q_nat,
        g_nat,
        g_t,
        x1,
        grad_mid,
        w_in,
        inverse,
        delta,
        norm_params,
        norm_two,
        head_two,
    )
    output, input_grad, grad_norm, *updates = finish(early, late, squares, state, out_all, grad_all, outputs)
    updates = [turn(v) if index in (0, 1, 2, 3, 9, 19) else v for index, v in enumerate(updates)]
    return (output, input_grad, grad_norm.reshape(()), *updates)


def solution(mesh):
    by_in, by_rows, by_cols = P(None, None, "narrow"), P("narrow", None), P(None, "narrow")
    kinds = (by_in, by_rows, by_cols, by_rows, P(), P())
    means = (
        P(None, "wide", "narrow"),
        P("narrow", "wide"),
        P("wide", "narrow"),
        P("narrow", "wide"),
        P(None, "wide"),
        P(None, "wide"),
    )
    cell = P("wide", None, None)
    outs = (cell, cell, P())
    for kind, mean in zip(kinds, means):
        outs += (kind, kind, kind, kind, mean)
    return jax.shard_map(
        on_device,
        mesh=mesh,
        in_specs=(cell, P("wide"), P("wide", None)) + kinds * 3 + means,
        out_specs=outs,
        check_vma=False,
    )
```
